32 devices in a mesh: ka: 4 (over y, x), pw: 8 (over z, core).
Axes of the slice: x: 2, y: 2, z: 4, core: 2. Of those that a mesh axis runs over, the one named last changes fastest.
Arguments:
- states_re: bfloat16 [8, 512, 32768], P('ka', None, 'pw'), may hold values from -0.016572815 to 0.016572815
- states_im: bfloat16 [8, 512, 32768], P('ka', None, 'pw'), may hold values from -0.016572815 to 0.016572815
Outputs:
- wilson_lines: float32 [8, 512, 2, 512], P('ka', 'pw')
The draws below stay inside these ranges and needn't reach their ends.
All inputs are finite; a program needn't handle non-finite values.
Results may differ from the reference program's by a relative error of at most 0.0003.
Values may be sent and summed in bfloat16 or wider, within the bound.
No kernel may reach another device: no remote copies, remote signals or barrier semaphores. Data moves between devices by JAX's collectives and lax.ppermute only.
A program may use at most 128 MiB of HBM per device.

```python
import math
import jax
import jax.numpy as jnp
from jax import lax

NB = 512
NPW = 32768
NK = 8


def state_parts(key):
    freqs = jax.random.permutation(jax.random.fold_in(key, 6), NPW)[:NB].astype(jnp.int32)
    waves = jnp.arange(NPW, dtype=jnp.int32)
    turns = freqs[:, None] * waves[None, :] % NPW
    phases = jax.random.uniform(jax.random.fold_in(key, 5), (NK, NB, 1), jnp.float32, -math.pi, math.pi)
    angle = 2.0 * math.pi / NPW * turns.astype(jnp.float32)[None, :, :] + phases
    noise_re = jnp.clip(jax.random.normal(jax.random.fold_in(key, 7), (NK, NB, NPW), jnp.float32), -4.0, 4.0)
    noise_im = jnp.clip(jax.random.normal(jax.random.fold_in(key, 8), (NK, NB, NPW), jnp.float32), -4.0, 4.0)
    noise_scale = 0.6 / math.sqrt(2.0 * NPW)
    base_scale = 1.0 / math.sqrt(NPW)
    return (base_scale * jnp.cos(angle) + noise_scale * noise_re, base_scale * jnp.sin(angle) + noise_scale * noise_im)


def draw_states_re(key, part):
    return state_parts(key)[0].astype(jnp.bfloat16)


def draw_states_im(key, part):
    return state_parts(key)[1].astype(jnp.bfloat16)


def setup_inputs(seed: int = 0) -> dict:
    arg_keys = jax.random.split(jax.random.key(seed), 3)
    states_re = draw_states_re(jax.random.fold_in(arg_keys[2], 71), 0)
    states_im = draw_states_im(jax.random.fold_in(arg_keys[2], 71), 0)
    return dict(states_re=states_re, states_im=states_im)


def complex_rows(left, right):
    highest = lax.Precision.HIGHEST
    left_re = left[:, 0]
    left_im = left[:, 1]
    right_re = right[:, 0]
    right_im = right[:, 1]
    real_part = jnp.dot(left_re, right_re, precision=highest, preferred_element_type=jnp.float32) - jnp.dot(left_im, right_im, precision=highest, preferred_element_type=jnp.float32)
    imag_part = jnp.dot(left_re, right_im, precision=highest, preferred_element_type=jnp.float32) + jnp.dot(left_im, right_re, precision=highest, preferred_element_type=jnp.float32)
    return jnp.stack([real_part, imag_part], 1)


def reference(states_re, states_im):
    highest = lax.Precision.HIGHEST

    def margin_at(kpoint):
        later = (kpoint + 1) % NK
        own_re = states_re[kpoint].astype(jnp.float32)
        own_im = states_im[kpoint].astype(jnp.float32)
        next_re = states_re[later].astype(jnp.float32)
        next_im = states_im[later].astype(jnp.float32)
        real_part = jnp.dot(own_re, next_re.T, precision=highest, preferred_element_type=jnp.float32) + jnp.dot(own_im, next_im.T, precision=highest, preferred_element_type=jnp.float32)
        imag_part = jnp.dot(own_re, next_im.T, precision=highest, preferred_element_type=jnp.float32) - jnp.dot(own_im, next_re.T, precision=highest, preferred_element_type=jnp.float32)
        return jnp.stack([real_part, imag_part], 1)

    margins = lax.map(margin_at, jnp.arange(NK, dtype=jnp.int32))
    identity = jnp.stack([jnp.eye(NB, dtype=jnp.float32), jnp.zeros((NB, NB), jnp.float32)], 1)

    def advance(carry, margin):
        line = complex_rows(carry, margin)
        return line, line

    final_line, lines = lax.scan(advance, identity, margins)
    return lines
```

```python
import jax
import jax.numpy as jnp
from jax import lax
from jax.sharding import PartitionSpec as P


def exact_dot(left, right):
    return jnp.dot(left, right, precision=lax.Precision.HIGH, preferred_element_type=jnp.float32)


def packed(states_re, states_im, kpoint, first, width):
    parts = [s[kpoint, first : first + width] for s in (states_re, states_im)]
    return jnp.concatenate(parts, 0)


def margin_of(own, other):
    bands = own.shape[0] // 2
    width = other.shape[0] // 2
    dots = lax.dot_general(own, other, (((1,), (1,)), ((), ())), preferred_element_type=jnp.float32)
    real_part = dots[:bands, :width] + dots[bands:, width:]
    imag_part = dots[:bands, width:] - dots[bands:, :width]
    return real_part, imag_part


def block_form(matrix):
    bands = matrix.shape[0]
    real_part, imag_part = matrix[:, :bands], matrix[:, bands:]
    return jnp.concatenate(
        [jnp.concatenate([real_part, -imag_part], 1), jnp.concatenate([imag_part, real_part], 1)], 0
    )


def rows_times(rows, matrix):
    _, count, bands = rows.shape
    dots = exact_dot(rows.reshape(2 * count, bands), matrix)
    real_part = dots[:count, :bands] - dots[count:, bands:]
    imag_part = dots[:count, bands:] + dots[count:, :bands]
    return jnp.stack([real_part, imag_part], 0)


def after(value, earlier):
    return lax.optimization_barrier((value, earlier))[0]


def shards(states_re, states_im):
    kcount, bands, _ = states_re.shape
    ka_width = lax.axis_size("ka")
    pw_width = lax.axis_size("pw")
    band_rows = bands // pw_width
    ka_place = lax.axis_index("ka")
    first_band = lax.axis_index("pw") * band_rows
    eighth = bands // 8
    widths = [eighth, 2 * eighth, 2 * eighth, 2 * eighth, eighth]
    firsts = [sum(widths[:i]) for i in range(len(widths))]

    to_previous = [(i, (i - 1) % ka_width) for i in range(ka_width)]
    arrivals = []
    for number, (first, width) in enumerate(zip(firsts, widths)):
        block = packed(states_re, states_im, 0, first, width)
        if number >= 2:
            block = after(block, arrivals[number - 2])
        arrivals.append(lax.ppermute(block, "ka", to_previous))

    states_re, states_im = after((states_re, states_im), arrivals[0])
    whole = [packed(states_re, states_im, k, 0, bands) for k in range(kcount)]
    own_margins = []
    before = None
    for k in range(kcount - 1):
        margin = lax.psum(jnp.concatenate(margin_of(whole[k], whole[k + 1]), 1), "pw")
        if before is not None:
            before = rows_times(jnp.stack([before[:, :bands], before[:, bands:]]), margin)
            margin = jnp.concatenate([before[0], before[1]], 1)
        before = margin
        own_margins.append(margin)
    left = None if before is None else block_form(after(before, arrivals[1]))

    sections = []
    last_dots = None
    for block in arrivals:
        if last_dots is not None:
            block = after(block, last_dots)
        real_part, imag_part = margin_of(whole[kcount - 1], block)
        last_dots = real_part
        if left is not None:
            product = exact_dot(left, jnp.concatenate([real_part, imag_part], 0))
            real_part, imag_part = product[:bands], product[bands:]
        section = jnp.concatenate([real_part, imag_part], 1)
        if sections:
            section = after(section, sections[-1])
        sections.append(lax.psum(section, "pw"))
    reals = [section[:, : section.shape[1] // 2] for section in sections]
    imags = [section[:, section.shape[1] // 2 :] for section in sections]
    span = jnp.concatenate(reals + imags, 1)

    line = lax.dynamic_slice_in_dim(span, first_band, band_rows, 0)
    line = jnp.stack([line[:, :bands], line[:, bands:]], 0)
    row_index = lax.broadcasted_iota(jnp.int32, (band_rows, bands), 0) + first_band
    col_index = lax.broadcasted_iota(jnp.int32, (band_rows, bands), 1)
    eye_real = (row_index == col_index).astype(jnp.float32)
    start = jnp.stack([eye_real, jnp.zeros_like(eye_real)], 0)
    for place in range(1, ka_width):
        received = lax.ppermute(line, "ka", [(place - 1, place)])
        start = jnp.where(ka_place == place, received, start)
        if place < ka_width - 1:
            line = rows_times(start, span)

    lines = [rows_times(start, matrix) for matrix in own_margins + [span]]
    return jnp.stack([jnp.moveaxis(one, 0, 1) for one in lines], 0)


def solution(mesh):
    in_specs = (P("ka", None, "pw"), P("ka", None, "pw"))
    out_specs = P("ka", "pw", None, None)
    return jax.shard_map(shards, mesh=mesh, in_specs=in_specs, out_specs=out_specs, check_vma=False)
```

```python
import jax
import jax.numpy as jnp
from jax import lax
from jax.sharding import PartitionSpec as P


def exact_dot(left, right):
    return jnp.dot(left, right, precision=lax.Precision.HIGH, preferred_element_type=jnp.float32)


def packed(states_re, states_im, kpoint, first, width):
    parts = [s[kpoint, first : first + width] for s in (states_re, states_im)]
    return jnp.concatenate(parts, 0)


def margin_of(own, other):
    bands = own.shape[0] // 2
    width = other.shape[0] // 2
    dots = lax.dot_general(own, other, (((1,), (1,)), ((), ())), preferred_element_type=jnp.float32)
    real_part = dots[:bands, :width] + dots[bands:, width:]
    imag_part = dots[:bands, width:] - dots[bands:, :width]
    return real_part, imag_part


def block_form(matrix):
    bands = matrix.shape[0]
    real_part, imag_part = matrix[:, :bands], matrix[:, bands:]
    return jnp.concatenate(
        [jnp.concatenate([real_part, -imag_part], 1), jnp.concatenate([imag_part, real_part], 1)], 0
    )


def rows_times(rows, pieces):
    _, count, bands = rows.shape
    flat = rows.reshape(2 * count, bands)
    reals, imags = [], []
    for piece in pieces:
        width = piece.shape[1] // 2
        dots = exact_dot(flat, piece)
        reals.append(dots[:count, :width] - dots[count:, width:])
        imags.append(dots[:count, width:] + dots[count:, :width])
    return jnp.stack([jnp.concatenate(reals, 1), jnp.concatenate(imags, 1)], 0)


def after(value, earlier):
    return lax.optimization_barrier((value, earlier))[0]


def other_core(block):
    size = lax.axis_size("pw")
    return lax.ppermute(block, "pw", [(i, i ^ 1) for i in range(size)])


def other_chip(block, distance):
    size = lax.axis_size("pw")
    return lax.ppermute(block, "pw", [(i, (i + 2 * distance) % size) for i in range(size)])


def take(blocks, place, axis):
    return lax.dynamic_index_in_dim(blocks, place, axis, keepdims=False)


def chosen(place, blocks):
    picked = blocks[0]
    for number, block in enumerate(blocks[1:], 1):
        picked = jnp.where(place == number, block, picked)
    return picked


def sum_to_rows(part):
    chips = lax.axis_size("pw") // 2
    chip, core = lax.axis_index("pw") // 2, lax.axis_index("pw") % 2
    blocks = part.reshape(chips, 2, part.shape[0] // (2 * chips), part.shape[1])
    half = take(blocks, core, 1) + other_core(take(blocks, 1 - core, 1))
    total = take(half, chip, 0)
    received = [other_chip(take(half, (chip + d) % chips, 0), d) for d in range(1, chips)]
    return sum(received, total)


def rows_to_whole(rows):
    chips = lax.axis_size("pw") // 2
    chip, core = lax.axis_index("pw") // 2, lax.axis_index("pw") % 2
    ring = [rows] + [other_chip(rows, d) for d in range(1, chips)]
    mine = jnp.stack([chosen((chip - place) % chips, ring) for place in range(chips)], 0)
    theirs = other_core(mine)
    first = jnp.where(core == 0, mine, theirs)
    second = jnp.where(core == 0, theirs, mine)
    return jnp.stack([first, second], 1).reshape(-1, rows.shape[1])


def shards(states_re, states_im):
    kcount, bands, _ = states_re.shape
    ka_width = lax.axis_size("ka")
    pw_width = lax.axis_size("pw")
    band_rows = bands // pw_width
    ka_place = lax.axis_index("ka")
    first_band = lax.axis_index("pw") * band_rows
    eighth = bands // 8
    little = bands // 32
    widths = [little, 2 * eighth - little, 2 * eighth, 2 * eighth, 2 * eighth]
    firsts = [sum(widths[:i]) for i in range(len(widths))]
    members = [[0, 1, 2, 3], [4]]

    to_previous = [(i, (i - 1) % ka_width) for i in range(ka_width)]
    arrivals = []
    for number, (first, width) in enumerate(zip(firsts, widths)):
        block = packed(states_re, states_im, 0, first, width)
        if number >= 2:
            block = after(block, arrivals[number - 2])
        arrivals.append(lax.ppermute(block, "ka", to_previous))

    states_re, states_im = after((states_re, states_im), arrivals[0])
    whole = [packed(states_re, states_im, k, 0, bands) for k in range(kcount)]
    own_margins = []
    before = None
    for k in range(kcount - 1):
        margin = lax.psum(jnp.concatenate(margin_of(whole[k], whole[k + 1]), 1), "pw")
        if before is not None:
            before = rows_times(jnp.stack([before[:, :bands], before[:, bands:]]), [margin])
            margin = jnp.concatenate([before[0], before[1]], 1)
        before = margin
        own_margins.append(margin)
    left = None if before is None else block_form(after(before, arrivals[1]))

    sections = []
    last_dots = None
    for group in members:
        parts = []
        for number in group:
            block = arrivals[number]
            if last_dots is not None:
                block = after(block, last_dots)
            parts.append(margin_of(whole[kcount - 1], block))
            last_dots = parts[-1][0]
        real_part, imag_part = (jnp.concatenate([p[i] for p in parts], 1) for i in (0, 1))
        if left is not None:
            product = exact_dot(left, jnp.concatenate([real_part, imag_part], 0))
            real_part, imag_part = product[:bands], product[bands:]
        section = jnp.concatenate([real_part, imag_part], 1)
        if number < len(widths) - 1:
            whole_section = lax.psum(section, "pw")
            rows = lax.dynamic_slice_in_dim(whole_section, first_band, band_rows, 0)
        else:
            rows = sum_to_rows(section)
            whole_section = rows_to_whole(rows)
        sections.append((rows, whole_section))
    spans = [whole_section for _, whole_section in sections]

    reals, imags = [], []
    for rows, _ in sections:
        width = rows.shape[1] // 2
        reals.append(rows[:, :width])
        imags.append(rows[:, width:])
    line = jnp.stack([jnp.concatenate(reals, 1), jnp.concatenate(imags, 1)], 0)
    row_index = lax.broadcasted_iota(jnp.int32, (band_rows, bands), 0) + first_band
    col_index = lax.broadcasted_iota(jnp.int32, (band_rows, bands), 1)
    eye_real = (row_index == col_index).astype(jnp.float32)
    start = jnp.stack([eye_real, jnp.zeros_like(eye_real)], 0)
    for place in range(1, ka_width):
        received = lax.ppermute(line, "ka", [(place - 1, place)])
        start = jnp.where(ka_place == place, received, start)
        if place < ka_width - 1:
            line = rows_times(start, spans)

    lines = [rows_times(start, [margin]) for margin in own_margins] + [rows_times(start, spans)]
    return jnp.stack([jnp.moveaxis(one, 0, 1) for one in lines], 0)


def solution(mesh):
    in_specs = (P("ka", None, "pw"), P("ka", None, "pw"))
    out_specs = P("ka", "pw", None, None)
    return jax.shard_map(shards, mesh=mesh, in_specs=in_specs, out_specs=out_specs, check_vma=False)
```

```python
import functools

import jax
import jax.numpy as jnp
from jax import lax
from jax.experimental import pallas as pl
from jax.experimental.pallas import tpu as pltpu
from jax.sharding import PartitionSpec as P

VMEM_LIMIT = 40 * 1024 * 1024


def halves_of(value):
    high = value.astype(jnp.bfloat16)
    return high, (value - high.astype(jnp.float32)).astype(jnp.bfloat16)


def dot(left, right, across=0):
    return lax.dot_general(left, right, (((1,), (across,)), ((), ())), preferred_element_type=jnp.float32)


def turned(value):
    width = value.shape[1] // 2
    return jnp.concatenate([-value[:, width:], value[:, :width]], 1)


def margin_kernel(steps, pieces, with_left, by_core, *refs):
    refs = list(refs)
    core = refs.pop(0) if by_core else None
    own_re, own_im = refs[:2]
    real_part = jnp.concatenate([ref[...] for ref in refs[2 : 2 + pieces]], 0)
    imag_part = jnp.concatenate([ref[...] for ref in refs[2 + pieces : 2 + 2 * pieces]], 0)
    refs = refs[2 + 2 * pieces :]
    left_high, left_low = refs[:2] if with_left else (None, None)
    outs, total = refs[2 if with_left else 0 : -1], refs[-1]
    step = pl.program_id(0)
    term = dot(own_re[...], jnp.concatenate([real_part, imag_part], 0), 1)
    term += dot(own_im[...], jnp.concatenate([imag_part, -real_part], 0), 1)

    @pl.when(step == 0)
    def _():
        total[...] = term

    @pl.when(step > 0)
    def _():
        total[...] += term

    @pl.when(step == steps - 1)
    def _():
        if with_left:
            bands = left_high.shape[0]
            value = total[...]
            product = jnp.zeros_like(value)
            for first, factor in ((0, value), (bands, turned(value))):
                high, low = halves_of(factor)
                columns = slice(first, first + bands)
                product += dot(left_high[:, columns], high)
                product += dot(left_high[:, columns], low)
                product += dot(left_low[:, columns], high)
            total[...] = product
        if by_core:
            mine, theirs = outs
            rows = mine.shape[1]
            for chip in range(mine.shape[0]):
                for out, which in ((mine, core[0]), (theirs, 1 - core[0])):
                    first = pl.multiple_of((2 * chip + which) * rows, rows)
                    out[chip] = total[pl.ds(first, rows), :]
        else:
            outs[0][...] = total[...]


def margin_section(states, kpoint, others=None, left=None, core=None):
    _, bands, waves = states[0].shape
    depth = min(512, waves)
    steps = waves // depth
    own = pl.BlockSpec((None, bands, depth), lambda step: (kpoint, 0, step))
    if others is None:
        width = bands
        other_specs = [pl.BlockSpec((None, bands, depth), lambda step: (kpoint + 1, 0, step))] * 2
        others = states
    else:
        widths = [other.shape[0] // 2 for other in others]
        width = sum(widths)
        other_specs = [pl.BlockSpec((one, depth), lambda step: (0, step)) for one in widths]
        other_specs += [pl.BlockSpec((one, depth), lambda step: (1, step)) for one in widths]
        others = [*others, *others]
    operands, specs = [*states, *others], [own, own, *other_specs]
    if left is not None:
        operands += left
        specs += [pl.BlockSpec((bands, 2 * bands), lambda step: (0, 0))] * 2
    if core is not None:
        operands = [core, *operands]
        specs = [pl.BlockSpec(memory_space=pltpu.SMEM), *specs]
        chips = lax.axis_size("pw") // 2
        shape = (chips, bands // (2 * chips), 2 * width)
        out_shape = [jax.ShapeDtypeStruct(shape, jnp.float32)] * 2
        out_specs = [pl.BlockSpec(shape, lambda step: (0, 0, 0))] * 2
    else:
        out_shape = jax.ShapeDtypeStruct((bands, 2 * width), jnp.float32)
        out_specs = pl.BlockSpec((bands, 2 * width), lambda step: (0, 0))
    return pl.pallas_call(
        functools.partial(margin_kernel, steps, len(other_specs) // 2, left is not None, core is not None),
        grid=(steps,),
        in_specs=specs,
        out_specs=out_specs,
        out_shape=out_shape,
        scratch_shapes=[pltpu.VMEM((bands, 2 * width), jnp.float32)],
        compiler_params=pltpu.CompilerParams(vmem_limit_bytes=VMEM_LIMIT),
        cost_estimate=pl.CostEstimate(flops=0, bytes_accessed=0, transcendentals=0),
    )(*operands)


def split_kernel(value, high, low):
    high[...], low[...] = halves_of(value[...])


def split(value):
    return pl.pallas_call(
        split_kernel,
        out_shape=[jax.ShapeDtypeStruct(value.shape, jnp.bfloat16)] * 2,
        compiler_params=pltpu.CompilerParams(vmem_limit_bytes=VMEM_LIMIT),
    )(value)


def rows_kernel(terms, counts, *refs):
    rows_refs, out = refs[:terms], refs[-1]
    pieces = list(refs[terms:-1])
    rows = rows_refs[0][...]
    for ref in rows_refs[1:]:
        rows = rows + ref[...]
    _, count, bands = rows.shape
    flat = jnp.concatenate([rows[0], rows[1]], 0)
    high, low = halves_of(flat)
    both = jnp.concatenate([high, low], 0)
    for number, how_many in enumerate(counts):
        first = 0
        for _ in range(how_many):
            piece_high, piece_low = halves_of(pieces.pop(0)[...])
            product = dot(both, piece_high)
            product = product[: 2 * count] + product[2 * count :] + dot(high, piece_low)
            width = product.shape[1] // 2
            columns = slice(first, first + width)
            out[number, 0, :, columns] = product[:count, :width] - product[count:, width:]
            out[number, 1, :, columns] = product[:count, width:] + product[count:, :width]
            first += width


def rows_times(rows_list, matrices):
    _, count, bands = rows_list[0].shape
    counts = [len(pieces) for pieces in matrices]
    pieces = [piece for pieces in matrices for piece in pieces]
    return pl.pallas_call(
        functools.partial(rows_kernel, len(rows_list), counts),
        out_shape=jax.ShapeDtypeStruct((len(matrices), 2, count, bands), jnp.float32),
        compiler_params=pltpu.CompilerParams(vmem_limit_bytes=VMEM_LIMIT),
        cost_estimate=pl.CostEstimate(
            flops=24 * count * bands * bands * len(matrices), bytes_accessed=8 * bands * bands, transcendentals=0
        ),
    )(*rows_list, *pieces)


def gather_kernel(*refs):
    out, first = refs[-1], 0
    for ref in refs[:-1]:
        width = ref.shape[1] // 2
        out[0, :, first : first + width] = ref[:, :width]
        out[1, :, first : first + width] = ref[:, width:]
        first += width


def stacked_rows(pieces):
    shape = (2, pieces[0].shape[0], sum(piece.shape[1] for piece in pieces) // 2)
    return pl.pallas_call(gather_kernel, out_shape=jax.ShapeDtypeStruct(shape, jnp.float32))(*pieces)


def packed(states, kpoint, first, width):
    return jnp.concatenate([s[kpoint, first : first + width] for s in states], 0)


def after(value, earlier):
    return lax.optimization_barrier((value, earlier))[0]


def other_core(block):
    size = lax.axis_size("pw")
    return lax.ppermute(block, "pw", [(i, i ^ 1) for i in range(size)])


def other_chip(block, distance):
    size = lax.axis_size("pw")
    return lax.ppermute(block, "pw", [(i, (i + 2 * distance) % size) for i in range(size)])


def chosen(place, blocks):
    picked = blocks[0]
    for number, block in enumerate(blocks[1:], 1):
        picked = jnp.where(place == number, block, picked)
    return picked


def sum_to_rows(mine, theirs):
    chips = mine.shape[0]
    chip = lax.axis_index("pw") // 2
    half = mine + other_core(theirs)

    def block(place):
        return lax.dynamic_index_in_dim(half, place % chips, 0, keepdims=False)

    received = [other_chip(block(chip + d), d) for d in range(1, chips)]
    return sum(received, block(chip))


def rows_to_whole(rows):
    chips = lax.axis_size("pw") // 2
    chip, core = lax.axis_index("pw") // 2, lax.axis_index("pw") % 2
    ring = [rows] + [other_chip(rows, d) for d in range(1, chips)]
    mine = jnp.stack([chosen((chip - place) % chips, ring) for place in range(chips)], 0)
    theirs = other_core(mine)
    first = jnp.where(core == 0, mine, theirs)
    second = jnp.where(core == 0, theirs, mine)
    return mine, jnp.stack([first, second], 1).reshape(-1, rows.shape[1])


def shards(states_re, states_im):
    kcount, bands, _ = states_re.shape
    ka_width = lax.axis_size("ka")
    pw_width = lax.axis_size("pw")
    band_rows = bands // pw_width
    ka_place = lax.axis_index("ka")
    first_band = lax.axis_index("pw") * band_rows
    core = (lax.axis_index("pw") % 2).reshape(1).astype(jnp.int32)
    quarter = bands // 4
    widths = [2 * quarter, quarter, quarter]
    firsts = [sum(widths[:i]) for i in range(len(widths))]
    to_previous = [(i, (i - 1) % ka_width) for i in range(ka_width)]
    blocks = [packed((states_re, states_im), 0, first, width) for first, width in zip(firsts, widths)]

    def send(number, *earlier):
        return lax.ppermute(after(blocks[number], earlier) if earlier else blocks[number], "ka", to_previous)

    arrivals = [send(0)]
    states = after((states_re, states_im), blocks[0])
    last = kcount - 1
    terms = [margin_section(states, k) for k in range(last)]
    arrivals.append(send(1, terms))
    own_margins = [lax.psum(term, "pw") for term in terms]
    before = own_margins[0]
    for k in range(1, last):
        rows = jnp.stack([before[:, :bands], before[:, bands:]], 0)
        before = rows_times([rows], [[own_margins[k]]])[0]
        before = jnp.concatenate([before[0], before[1]], 1)
        own_margins[k] = before
    left = split(after(before, arrivals[0]))

    rows, span = [], []
    for number in range(len(widths)):
        piece = arrivals[number]
        if number > 0:
            piece = after(piece, half)
        mine, theirs = margin_section(states, last, [piece], left, core)
        if number == 0:
            arrivals.append(send(2, arrivals[0], mine))
        rows.append(sum_to_rows(mine, theirs))
        half, section = rows_to_whole(rows[-1])
        span.append(section)

    line = stacked_rows(rows)
    row_index = lax.broadcasted_iota(jnp.int32, (band_rows, bands), 0) + first_band
    col_index = lax.broadcasted_iota(jnp.int32, (band_rows, bands), 1)
    eye_real = jnp.where((row_index == col_index) & (ka_place == 0), 1.0, 0.0).astype(jnp.float32)
    starts = [jnp.stack([eye_real, jnp.zeros_like(eye_real)], 0)]
    for place in range(1, ka_width):
        starts.append(lax.ppermute(line, "ka", [(place - 1, place)]))
        if place < ka_width - 1:
            line = rows_times([starts[-1]], [span])[0]

    lines = rows_times(starts, [[margin] for margin in own_margins] + [span])
    return jnp.moveaxis(lines, 1, 2)


def solution(mesh):
    in_specs = (P("ka", None, "pw"), P("ka", None, "pw"))
    out_specs = P("ka", "pw", None, None)
    return jax.shard_map(shards, mesh=mesh, in_specs=in_specs, out_specs=out_specs, check_vma=False)
```

```python
import functools

import jax
import jax.numpy as jnp
from jax import lax
from jax.experimental import pallas as pl
from jax.experimental.pallas import tpu as pltpu
from jax.sharding import PartitionSpec as P

VMEM_LIMIT = 40 * 1024 * 1024


def halves_of(value):
    high = value.astype(jnp.bfloat16)
    return high, (value - high.astype(jnp.float32)).astype(jnp.bfloat16)


def dot(left, right, across=0):
    return lax.dot_general(left, right, (((1,), (across,)), ((), ())), preferred_element_type=jnp.float32)


def turned(value):
    width = value.shape[1] // 2
    return jnp.concatenate([-value[:, width:], value[:, :width]], 1)


def margin_kernel(steps, pieces, with_left, by_core, *refs):
    refs = list(refs)
    core = refs.pop(0) if by_core else None
    own_re, own_im = refs[:2]
    real_part = jnp.concatenate([ref[...] for ref in refs[2 : 2 + pieces]], 0)
    imag_part = jnp.concatenate([ref[...] for ref in refs[2 + pieces : 2 + 2 * pieces]], 0)
    refs = refs[2 + 2 * pieces :]
    left_high, left_low = refs[:2] if with_left else (None, None)
    outs, total = refs[2 if with_left else 0 : -1], refs[-1]
    step = pl.program_id(0)
    other = jnp.concatenate([jnp.concatenate([real_part, imag_part], 1), jnp.concatenate([imag_part, -real_part], 1)], 0)
    term = dot(jnp.concatenate([own_re[...], own_im[...]], 1), other, 1)

    @pl.when(step == 0)
    def _():
        total[...] = term

    @pl.when(step > 0)
    def _():
        total[...] += term

    @pl.when(step == steps - 1)
    def _():
        if with_left:
            bands = left_high.shape[0]
            value = total[...]
            product = jnp.zeros_like(value)
            for first, factor in ((0, value), (bands, turned(value))):
                high, low = halves_of(factor)
                columns = slice(first, first + bands)
                product += dot(left_high[:, columns], high)
                product += dot(left_high[:, columns], low)
                product += dot(left_low[:, columns], high)
            total[...] = product
        if by_core:
            mine, theirs = outs
            rows = mine.shape[1]
            for chip in range(mine.shape[0]):
                for out, which in ((mine, core[0]), (theirs, 1 - core[0])):
                    first = pl.multiple_of((2 * chip + which) * rows, rows)
                    out[chip] = total[pl.ds(first, rows), :]
        else:
            outs[0][...] = total[...]


def margin_section(states, kpoint, others=None, left=None, core=None):
    _, bands, waves = states[0].shape
    depth = min(1024, waves)
    steps = waves // depth
    own = pl.BlockSpec((None, bands, depth), lambda step: (kpoint, 0, step))
    if others is None:
        width = bands
        other_specs = [pl.BlockSpec((None, bands, depth), lambda step: (kpoint + 1, 0, step))] * 2
        others = states
    else:
        widths = [other.shape[0] // 2 for other in others]
        width = sum(widths)
        other_specs = [pl.BlockSpec((one, depth), lambda step: (0, step)) for one in widths]
        other_specs += [pl.BlockSpec((one, depth), lambda step: (1, step)) for one in widths]
        others = [*others, *others]
    operands, specs = [*states, *others], [own, own, *other_specs]
    if left is not None:
        operands += left
        specs += [pl.BlockSpec((bands, 2 * bands), lambda step: (0, 0))] * 2
    if core is not None:
        operands = [core, *operands]
        specs = [pl.BlockSpec(memory_space=pltpu.SMEM), *specs]
        chips = lax.axis_size("pw") // 2
        shape = (chips, bands // (2 * chips), 2 * width)
        out_shape = [jax.ShapeDtypeStruct(shape, jnp.float32)] * 2
        out_specs = [pl.BlockSpec(shape, lambda step: (0, 0, 0))] * 2
    else:
        out_shape = jax.ShapeDtypeStruct((bands, 2 * width), jnp.float32)
        out_specs = pl.BlockSpec((bands, 2 * width), lambda step: (0, 0))
    return pl.pallas_call(
        functools.partial(margin_kernel, steps, len(other_specs) // 2, left is not None, core is not None),
        grid=(steps,),
        in_specs=specs,
        out_specs=out_specs,
        out_shape=out_shape,
        scratch_shapes=[pltpu.VMEM((bands, 2 * width), jnp.float32)],
        compiler_params=pltpu.CompilerParams(vmem_limit_bytes=VMEM_LIMIT),
        cost_estimate=pl.CostEstimate(flops=0, bytes_accessed=0, transcendentals=0),
    )(*operands)


def split_kernel(value, high, low):
    high[...], low[...] = halves_of(value[...])


def split(value):
    return pl.pallas_call(
        split_kernel,
        out_shape=[jax.ShapeDtypeStruct(value.shape, jnp.bfloat16)] * 2,
        compiler_params=pltpu.CompilerParams(vmem_limit_bytes=VMEM_LIMIT),
    )(value)


def next_piece(refs):
    ref = refs.pop(0)
    return (ref[...], refs.pop(0)[...]) if ref.dtype == jnp.bfloat16 else halves_of(ref[...])


def rows_kernel(terms, counts, *refs):
    rows_refs, out = refs[:terms], refs[-1]
    pieces = list(refs[terms:-1])
    rows = rows_refs[0][...]
    for ref in rows_refs[1:]:
        rows = rows + ref[...]
    _, count, bands = rows.shape
    flat = jnp.concatenate([rows[0], rows[1]], 0)
    high, low = halves_of(flat)
    both = jnp.concatenate([high, low], 0)
    for number, how_many in enumerate(counts):
        first = 0
        for _ in range(how_many):
            piece_high, piece_low = next_piece(pieces)
            product = dot(both, piece_high)
            product = product[: 2 * count] + product[2 * count :] + dot(high, piece_low)
            width = product.shape[1] // 2
            columns = slice(first, first + width)
            out[number, 0, :, columns] = product[:count, :width] - product[count:, width:]
            out[number, 1, :, columns] = product[:count, width:] + product[count:, :width]
            first += width


def rows_times(rows_list, matrices):
    _, count, bands = rows_list[0].shape
    counts = [len(pieces) for pieces in matrices]
    pieces = jax.tree.leaves(matrices)
    return pl.pallas_call(
        functools.partial(rows_kernel, len(rows_list), counts),
        out_shape=jax.ShapeDtypeStruct((len(matrices), 2, count, bands), jnp.float32),
        compiler_params=pltpu.CompilerParams(vmem_limit_bytes=VMEM_LIMIT),
        cost_estimate=pl.CostEstimate(
            flops=24 * count * bands * bands * len(matrices), bytes_accessed=8 * bands * bands, transcendentals=0
        ),
    )(*rows_list, *pieces)


def gather_kernel(*refs):
    out, first = refs[-1], 0
    for ref in refs[:-1]:
        width = ref.shape[1] // 2
        out[0, :, first : first + width] = ref[:, :width]
        out[1, :, first : first + width] = ref[:, width:]
        first += width


def stacked_rows(pieces):
    shape = (2, pieces[0].shape[0], sum(piece.shape[1] for piece in pieces) // 2)
    return pl.pallas_call(gather_kernel, out_shape=jax.ShapeDtypeStruct(shape, jnp.float32))(*pieces)


def pack_kernel(kpoint, first, width, parts, re_ref, im_ref, out, sems):
    copies = []
    step = width // parts
    for part in range(parts):
        for half, ref in enumerate((re_ref, im_ref)):
            source = ref.at[kpoint, pl.ds(first + part * step, step), :]
            target = out.at[pl.ds(half * width + part * step, step), :]
            copies.append(pltpu.make_async_copy(source, target, sems.at[len(copies)]))
            copies[-1].start()
    for copy in copies:
        copy.wait()


def packed(states, kpoint, first, width):
    parts = max(1, min(8, width // 16))
    return pl.pallas_call(
        functools.partial(pack_kernel, kpoint, first, width, parts),
        in_specs=[pl.BlockSpec(memory_space=pl.ANY)] * 2,
        out_specs=pl.BlockSpec(memory_space=pl.ANY),
        out_shape=jax.ShapeDtypeStruct((2 * width, states[0].shape[2]), states[0].dtype),
        scratch_shapes=[pltpu.SemaphoreType.DMA((2 * parts,))],
        compiler_params=pltpu.CompilerParams(vmem_limit_bytes=60 * 1024 * 1024),
    )(*states)


def after(value, earlier):
    return lax.optimization_barrier((value, earlier))[0]


def other_core(block):
    size = lax.axis_size("pw")
    return lax.ppermute(block, "pw", [(i, i ^ 1) for i in range(size)])


def other_chip(block, distance):
    size = lax.axis_size("pw")
    return lax.ppermute(block, "pw", [(i, (i + 2 * distance) % size) for i in range(size)])


def chosen(place, blocks):
    picked = blocks[0]
    for number, block in enumerate(blocks[1:], 1):
        picked = jnp.where(place == number, block, picked)
    return picked


def sum_to_rows(mine, theirs):
    chips = mine.shape[0]
    chip = lax.axis_index("pw") // 2
    half = mine + other_core(theirs)

    def block(place):
        return lax.dynamic_index_in_dim(half, place % chips, 0, keepdims=False)

    received = [other_chip(block(chip + d), d) for d in range(1, chips)]
    return sum(received, block(chip))


def rows_to_core(rows):
    chips = lax.axis_size("pw") // 2
    chip = lax.axis_index("pw") // 2
    ring = [rows] + [other_chip(rows, d) for d in range(1, chips)]
    return jnp.stack([chosen((chip - place) % chips, ring) for place in range(chips)], 0)


def core_to_whole(mine):
    core = lax.axis_index("pw") % 2
    theirs = other_core(mine)
    first = jnp.where(core == 0, mine, theirs)
    second = jnp.where(core == 0, theirs, mine)
    return jnp.stack([first, second], 1).reshape(-1, mine.shape[2])


def shards(states_re, states_im):
    kcount, bands, _ = states_re.shape
    ka_width = lax.axis_size("ka")
    pw_width = lax.axis_size("pw")
    band_rows = bands // pw_width
    ka_place = lax.axis_index("ka")
    first_band = lax.axis_index("pw") * band_rows
    core = (lax.axis_index("pw") % 2).reshape(1).astype(jnp.int32)
    quarter = bands // 4
    widths = [2 * quarter, quarter, quarter]
    firsts = [sum(widths[:i]) for i in range(len(widths))]
    to_previous = [(i, (i - 1) % ka_width) for i in range(ka_width)]
    blocks = [packed((states_re, states_im), 0, first, width) for first, width in zip(firsts, widths)]

    def send(number, *earlier):
        return lax.ppermute(after(blocks[number], earlier) if earlier else blocks[number], "ka", to_previous)

    arrivals = [send(0)]
    states = after((states_re, states_im), blocks[0])
    last = kcount - 1
    terms = [margin_section(states, k) for k in range(last)]
    arrivals.append(send(1, terms))
    own_margins = [lax.psum(term, "pw") for term in terms]
    before = own_margins[0]
    for k in range(1, last):
        rows = jnp.stack([before[:, :bands], before[:, bands:]], 0)
        before = rows_times([rows], [[own_margins[k]]])[0]
        before = jnp.concatenate([before[0], before[1]], 1)
        own_margins[k] = before
    left = split(after(before, arrivals[0]))

    rows, span = [], []
    for number in range(len(widths)):
        piece = arrivals[number]
        if number > 0:
            piece = after(piece, half)
        mine, theirs = margin_section(states, last, [piece], left, core)
        if number == 0:
            arrivals.append(send(2, arrivals[0], mine))
        rows.append(sum_to_rows(mine, theirs))
        half = rows_to_core(rows[-1])
        if number < len(widths) - 1:
            span.append(core_to_whole(half))
    received = lax.ppermute(stacked_rows(rows), "ka", [(0, 1)])
    span.append(core_to_whole(after(half, received)))

    row_index = lax.broadcasted_iota(jnp.int32, (band_rows, bands), 0) + first_band
    col_index = lax.broadcasted_iota(jnp.int32, (band_rows, bands), 1)
    eye_real = jnp.where((row_index == col_index) & (ka_place == 0), 1.0, 0.0).astype(jnp.float32)
    starts = [jnp.stack([eye_real, jnp.zeros_like(eye_real)], 0)]
    starts.append(received)
    for place in range(1, ka_width - 1):
        line = rows_times([starts[-1]], [span])[0]
        starts.append(lax.ppermute(line, "ka", [(place, place + 1)]))

    margins = [[margin] for margin in own_margins]
    margins[-1] = [left]
    lines = rows_times(starts, margins + [span])
    return jnp.moveaxis(lines, 1, 2)


def solution(mesh):
    in_specs = (P("ka", None, "pw"), P("ka", None, "pw"))
    out_specs = P("ka", "pw", None, None)
    return jax.shard_map(shards, mesh=mesh, in_specs=in_specs, out_specs=out_specs, check_vma=False)
```

```python
import functools

import jax
import jax.numpy as jnp
from jax import lax
from jax.experimental import pallas as pl
from jax.experimental.pallas import tpu as pltpu
from jax.sharding import PartitionSpec as P

VMEM_LIMIT = 40 * 1024 * 1024


def halves_of(value):
    high = value.astype(jnp.bfloat16)
    return high, (value - high.astype(jnp.float32)).astype(jnp.bfloat16)


def dot(left, right, across=0):
    return lax.dot_general(left, right, (((1,), (across,)), ((), ())), preferred_element_type=jnp.float32)


def turned(value):
    width = value.shape[1] // 2
    return jnp.concatenate([-value[:, width:], value[:, :width]], 1)


def margin_kernel(steps, pieces, with_left, by_core, *refs):
    refs = list(refs)
    core = refs.pop(0) if by_core else None
    own_re, own_im = refs[:2]
    real_part = jnp.concatenate([ref[...] for ref in refs[2 : 2 + pieces]], 0)
    imag_part = jnp.concatenate([ref[...] for ref in refs[2 + pieces : 2 + 2 * pieces]], 0)
    refs = refs[2 + 2 * pieces :]
    left_high, left_low = refs[:2] if with_left else (None, None)
    outs, total = refs[2 if with_left else 0 : -1], refs[-1]
    step = pl.program_id(0)
    other = jnp.concatenate([jnp.concatenate([real_part, imag_part], 1), jnp.concatenate([imag_part, -real_part], 1)], 0)
    term = dot(jnp.concatenate([own_re[...], own_im[...]], 1), other, 1)

    @pl.when(step == 0)
    def _():
        total[...] = term

    @pl.when(step > 0)
    def _():
        total[...] += term

    @pl.when(step == steps - 1)
    def _():
        if with_left:
            bands = left_high.shape[0]
            value = total[...]
            product = jnp.zeros_like(value)
            for first, factor in ((0, value), (bands, turned(value))):
                high, low = halves_of(factor)
                columns = slice(first, first + bands)
                product += dot(left_high[:, columns], high)
                product += dot(left_high[:, columns], low)
                product += dot(left_low[:, columns], high)
            total[...] = product
        if by_core:
            mine, theirs = outs
            rows = mine.shape[1]
            for chip in range(mine.shape[0]):
                for out, which in ((mine, core[0]), (theirs, 1 - core[0])):
                    first = pl.multiple_of((2 * chip + which) * rows, rows)
                    out[chip] = total[pl.ds(first, rows), :]
        else:
            outs[0][...] = total[...]


def margin_section(states, kpoint, others=None, left=None, core=None):
    _, bands, waves = states[0].shape
    depth = min(1024, waves)
    steps = waves // depth
    own = pl.BlockSpec((None, bands, depth), lambda step: (kpoint, 0, step))
    if others is None:
        width = bands
        other_specs = [pl.BlockSpec((None, bands, depth), lambda step: (kpoint + 1, 0, step))] * 2
        others = states
    else:
        widths = [other.shape[0] // 2 for other in others]
        width = sum(widths)
        other_specs = [pl.BlockSpec((one, depth), lambda step: (0, step)) for one in widths]
        other_specs += [pl.BlockSpec((one, depth), lambda step: (1, step)) for one in widths]
        others = [*others, *others]
    operands, specs = [*states, *others], [own, own, *other_specs]
    if left is not None:
        operands += left
        specs += [pl.BlockSpec((bands, 2 * bands), lambda step: (0, 0))] * 2
    if core is not None:
        operands = [core, *operands]
        specs = [pl.BlockSpec(memory_space=pltpu.SMEM), *specs]
        chips = lax.axis_size("pw") // 2
        shape = (chips, bands // (2 * chips), 2 * width)
        out_shape = [jax.ShapeDtypeStruct(shape, jnp.float32)] * 2
        out_specs = [pl.BlockSpec(shape, lambda step: (0, 0, 0))] * 2
    else:
        out_shape = jax.ShapeDtypeStruct((bands, 2 * width), jnp.float32)
        out_specs = pl.BlockSpec((bands, 2 * width), lambda step: (0, 0))
    return pl.pallas_call(
        functools.partial(margin_kernel, steps, len(other_specs) // 2, left is not None, core is not None),
        grid=(steps,),
        in_specs=specs,
        out_specs=out_specs,
        out_shape=out_shape,
        scratch_shapes=[pltpu.VMEM((bands, 2 * width), jnp.float32)],
        compiler_params=pltpu.CompilerParams(vmem_limit_bytes=VMEM_LIMIT),
        cost_estimate=pl.CostEstimate(flops=0, bytes_accessed=0, transcendentals=0),
    )(*operands)


def split_kernel(value, high, low):
    high[...], low[...] = halves_of(value[...])


def split(value):
    return pl.pallas_call(
        split_kernel,
        out_shape=[jax.ShapeDtypeStruct(value.shape, jnp.bfloat16)] * 2,
        compiler_params=pltpu.CompilerParams(vmem_limit_bytes=VMEM_LIMIT),
    )(value)


def whole_rows(term):
    if len(term) == 1 and len(term[0].shape) == 3:
        rows = term[0][...]
        return jnp.concatenate([rows[0], rows[1]], 0)
    widths = [ref.shape[1] // 2 for ref in term]
    reals = [ref[:, :width] for ref, width in zip(term, widths)]
    imags = [ref[:, width:] for ref, width in zip(term, widths)]
    return jnp.concatenate([jnp.concatenate(reals, 1), jnp.concatenate(imags, 1)], 0)


def whole_piece(refs, place):
    if refs[0].dtype == jnp.bfloat16:
        return refs[0][...], refs[1][...]
    if len(refs) == 1:
        return halves_of(refs[0][...])
    mine, theirs = refs
    chips = mine.shape[0]
    blocks = []
    for chip in range(chips):
        turn = lax.rem(place[0] - chip + chips, chips)
        one, other = mine[turn], theirs[turn]
        blocks += [jnp.where(place[1] == 0, one, other), jnp.where(place[1] == 0, other, one)]
    return halves_of(jnp.concatenate(blocks, 0))


def rows_kernel(tree, place, *refs):
    out = refs[-1]
    terms, matrices = jax.tree.unflatten(tree, refs[:-1])
    flat = whole_rows(terms[0])
    for term in terms[1:]:
        flat = flat + whole_rows(term)
    count = flat.shape[0] // 2
    high, low = halves_of(flat)
    both = jnp.concatenate([high, low], 0)
    for number, matrix in enumerate(matrices):
        first = 0
        for piece in matrix:
            piece_high, piece_low = whole_piece(piece, place)
            product = dot(both, piece_high)
            product = product[: 2 * count] + product[2 * count :] + dot(high, piece_low)
            width = product.shape[1] // 2
            columns = slice(first, first + width)
            out[number, 0, :, columns] = product[:count, :width] - product[count:, width:]
            out[number, 1, :, columns] = product[:count, width:] + product[count:, :width]
            first += width


def rows_times(place, terms, matrices, count, bands):
    flat, tree = jax.tree.flatten((terms, matrices))
    return pl.pallas_call(
        functools.partial(rows_kernel, tree),
        in_specs=[pl.BlockSpec(memory_space=pltpu.SMEM)] + [pl.BlockSpec(memory_space=pltpu.VMEM)] * len(flat),
        out_shape=jax.ShapeDtypeStruct((len(matrices), 2, count, bands), jnp.float32),
        compiler_params=pltpu.CompilerParams(vmem_limit_bytes=24 * 1024 * 1024),
        cost_estimate=pl.CostEstimate(flops=0, bytes_accessed=0, transcendentals=0),
    )(place, *flat)


def pack_kernel(re_ref, im_ref, out):
    out[0] = re_ref[...]
    out[1] = im_ref[...]


def packed_now(states, kpoint, width):
    waves = states[0].shape[2]
    step = min(32, width)
    return pl.pallas_call(
        pack_kernel,
        grid=(width // step,),
        in_specs=[pl.BlockSpec((None, step, waves), lambda i: (kpoint, i, 0))] * 2,
        out_specs=pl.BlockSpec((2, step, waves), lambda i: (0, i, 0)),
        out_shape=jax.ShapeDtypeStruct((2, width, waves), states[0].dtype),
        compiler_params=pltpu.CompilerParams(vmem_limit_bytes=60 * 1024 * 1024),
    )(*states).reshape(2 * width, waves)


def packed(states, kpoint, first, width):
    return jnp.concatenate([s[kpoint, first : first + width] for s in states], 0)


def after(value, earlier):
    return lax.optimization_barrier((value, earlier))[0]


def other_core(block):
    size = lax.axis_size("pw")
    return lax.ppermute(block, "pw", [(i, i ^ 1) for i in range(size)])


def other_chip(block, distance):
    size = lax.axis_size("pw")
    return lax.ppermute(block, "pw", [(i, (i + 2 * distance) % size) for i in range(size)])


def sum_to_rows(mine, theirs):
    chips = mine.shape[0]
    chip = lax.axis_index("pw") // 2
    half = mine + other_core(theirs)

    def block(place):
        return lax.dynamic_index_in_dim(half, place % chips, 0, keepdims=False)

    received = [other_chip(block(chip + d), d) for d in range(1, chips)]
    return sum(received, block(chip))


def rows_to_core(rows):
    chips = lax.axis_size("pw") // 2
    return jnp.stack([rows] + [other_chip(rows, d) for d in range(1, chips)], 0)


def shards(states_re, states_im):
    kcount, bands, _ = states_re.shape
    ka_width = lax.axis_size("ka")
    pw_width = lax.axis_size("pw")
    band_rows = bands // pw_width
    ka_place = lax.axis_index("ka")
    first_band = lax.axis_index("pw") * band_rows
    core = (lax.axis_index("pw") % 2).reshape(1).astype(jnp.int32)
    place = jnp.stack([lax.axis_index("pw") // 2, lax.axis_index("pw") % 2]).astype(jnp.int32)
    quarter = bands // 4
    widths = [2 * quarter, quarter, quarter]
    firsts = [sum(widths[:i]) for i in range(len(widths))]
    to_previous = [(i, (i - 1) % ka_width) for i in range(ka_width)]
    blocks = [packed_now((states_re, states_im), 0, widths[0])]
    blocks += [packed((states_re, states_im), 0, first, width) for first, width in zip(firsts[1:], widths[1:])]

    def send(number, *earlier):
        return lax.ppermute(after(blocks[number], earlier) if earlier else blocks[number], "ka", to_previous)

    arrivals = [send(0)]
    states = after((states_re, states_im), blocks[0])
    last = kcount - 1
    terms = [margin_section(states, k) for k in range(last)]
    arrivals.append(send(1, terms))
    own_margins = [lax.psum(term, "pw") for term in terms]
    before = own_margins[0]
    for k in range(1, last):
        rows = jnp.stack([before[:, :bands], before[:, bands:]], 0)
        before = rows_times(place, [[rows]], [[[own_margins[k]]]], bands, bands)[0]
        before = jnp.concatenate([before[0], before[1]], 1)
        own_margins[k] = before
    left = split(after(before, arrivals[0]))

    rows, span = [], []
    for number in range(len(widths)):
        piece = arrivals[number]
        if number > 0:
            piece = after(piece, half)
        mine, theirs = margin_section(states, last, [piece], left, core)
        if number == 0:
            arrivals.append(send(2, arrivals[0], mine))
        rows.append(sum_to_rows(mine, theirs))
        if number == len(widths) - 1:
            ready = lax.ppermute(after(tuple(rows[:-1]), piece), "ka", [(0, 1)])
            half = rows_to_core(after(rows[-1], ready))
            received = [*ready, lax.ppermute(rows[-1], "ka", [(0, 1)])]
            half_ready = after(half, received[-1])
        else:
            half = half_ready = rows_to_core(rows[-1])
        span.append([half_ready, other_core(half_ready)])

    row_index = lax.broadcasted_iota(jnp.int32, (band_rows, bands), 0) + first_band
    col_index = lax.broadcasted_iota(jnp.int32, (band_rows, bands), 1)
    eye_real = jnp.where((row_index == col_index) & (ka_place == 0), 1.0, 0.0).astype(jnp.float32)
    starts = [[jnp.stack([eye_real, jnp.zeros_like(eye_real)], 0)], received]
    for number in range(1, ka_width - 1):
        line = rows_times(place, starts[-1:], [span], band_rows, bands)[0]
        starts.append([lax.ppermute(line, "ka", [(number, number + 1)])])

    margins = [[[margin]] for margin in own_margins]
    margins[-1] = [left]
    lines = rows_times(place, starts, margins + [span], band_rows, bands)
    return jnp.moveaxis(lines, 1, 2)


def solution(mesh):
    in_specs = (P("ka", None, "pw"), P("ka", None, "pw"))
    out_specs = P("ka", "pw", None, None)
    return jax.shard_map(shards, mesh=mesh, in_specs=in_specs, out_specs=out_specs, check_vma=False)
```

```python
import functools

import jax
import jax.numpy as jnp
from jax import lax
from jax.experimental import pallas as pl
from jax.experimental.pallas import tpu as pltpu
from jax.sharding import PartitionSpec as P

VMEM_LIMIT = 40 * 1024 * 1024


def halves_of(value):
    high = value.astype(jnp.bfloat16)
    return high, (value - high.astype(jnp.float32)).astype(jnp.bfloat16)


def dot(left, right, across=0):
    return lax.dot_general(left, right, (((1,), (across,)), ((), ())), preferred_element_type=jnp.float32)


def turned(value):
    width = value.shape[1] // 2
    return jnp.concatenate([-value[:, width:], value[:, :width]], 1)


def margin_kernel(steps, pieces, with_left, by_core, *refs):
    refs = list(refs)
    core = refs.pop(0) if by_core else None
    own_re, own_im = refs[:2]
    real_part = jnp.concatenate([ref[...] for ref in refs[2 : 2 + pieces]], 0)
    imag_part = jnp.concatenate([ref[...] for ref in refs[2 + pieces : 2 + 2 * pieces]], 0)
    refs = refs[2 + 2 * pieces :]
    left_high, left_low = refs[:2] if with_left else (None, None)
    outs, total = refs[2 if with_left else 0 : -1], refs[-1]
    step = pl.program_id(0)
    other = jnp.concatenate([jnp.concatenate([real_part, imag_part], 1), jnp.concatenate([imag_part, -real_part], 1)], 0)
    term = dot(jnp.concatenate([own_re[...], own_im[...]], 1), other, 1)

    @pl.when(step == 0)
    def _():
        total[...] = term

    @pl.when(step > 0)
    def _():
        total[...] += term

    @pl.when(step == steps - 1)
    def _():
        if with_left:
            bands = left_high.shape[0]
            value = total[...]
            product = jnp.zeros_like(value)
            for first, factor in ((0, value), (bands, turned(value))):
                high, low = halves_of(factor)
                columns = slice(first, first + bands)
                product += dot(left_high[:, columns], high)
                product += dot(left_high[:, columns], low)
                product += dot(left_low[:, columns], high)
            total[...] = product
        if by_core:
            mine, theirs = outs
            rows = mine.shape[1]
            for chip in range(mine.shape[0]):
                for out, which in ((mine, core[0]), (theirs, 1 - core[0])):
                    first = pl.multiple_of((2 * chip + which) * rows, rows)
                    out[chip] = total[pl.ds(first, rows), :]
        else:
            outs[0][...] = total[...]


def margin_section(states, kpoint, others=None, left=None, core=None):
    _, bands, waves = states[0].shape
    depth = min(1024, waves)
    steps = waves // depth
    own = pl.BlockSpec((None, bands, depth), lambda step: (kpoint, 0, step))
    if others is None:
        width = bands
        other_specs = [pl.BlockSpec((None, bands, depth), lambda step: (kpoint + 1, 0, step))] * 2
        others = states
    else:
        packs = [other if isinstance(other, tuple) else (other, other) for other in others]
        apart = [isinstance(other, tuple) for other in others]
        widths = [pack[0].shape[0] // (1 if one else 2) for pack, one in zip(packs, apart)]
        width = sum(widths)
        other_specs = [pl.BlockSpec((one, depth), lambda step: (0, step)) for one in widths]
        for one, alone in zip(widths, apart):
            other_specs.append(pl.BlockSpec((one, depth), functools.partial(lambda row, step: (row, step), 0 if alone else 1)))
        others = [pack[0] for pack in packs] + [pack[1] for pack in packs]
    operands, specs = [*states, *others], [own, own, *other_specs]
    if left is not None:
        operands += left
        specs += [pl.BlockSpec((bands, 2 * bands), lambda step: (0, 0))] * 2
    if core is not None:
        operands = [core, *operands]
        specs = [pl.BlockSpec(memory_space=pltpu.SMEM), *specs]
        chips = lax.axis_size("pw") // 2
        shape = (chips, bands // (2 * chips), 2 * width)
        out_shape = [jax.ShapeDtypeStruct(shape, jnp.float32)] * 2
        out_specs = [pl.BlockSpec(shape, lambda step: (0, 0, 0))] * 2
    else:
        out_shape = jax.ShapeDtypeStruct((bands, 2 * width), jnp.float32)
        out_specs = pl.BlockSpec((bands, 2 * width), lambda step: (0, 0))
    return pl.pallas_call(
        functools.partial(margin_kernel, steps, len(other_specs) // 2, left is not None, core is not None),
        grid=(steps,),
        in_specs=specs,
        out_specs=out_specs,
        out_shape=out_shape,
        scratch_shapes=[pltpu.VMEM((bands, 2 * width), jnp.float32)],
        compiler_params=pltpu.CompilerParams(vmem_limit_bytes=VMEM_LIMIT),
        cost_estimate=pl.CostEstimate(flops=0, bytes_accessed=0, transcendentals=0),
    )(*operands)


def split_kernel(value, high, low):
    high[...], low[...] = halves_of(value[...])


def split(value):
    return pl.pallas_call(
        split_kernel,
        out_specs=[pl.BlockSpec(memory_space=pltpu.VMEM)] * 2,
        out_shape=[jax.ShapeDtypeStruct(value.shape, jnp.bfloat16)] * 2,
        compiler_params=pltpu.CompilerParams(vmem_limit_bytes=12 * 1024 * 1024),
    )(value)


def whole_rows(term):
    if len(term) == 1 and len(term[0].shape) == 3:
        rows = term[0][...]
        return jnp.concatenate([rows[0], rows[1]], 0)
    widths = [ref.shape[1] // 2 for ref in term]
    reals = [ref[:, :width] for ref, width in zip(term, widths)]
    imags = [ref[:, width:] for ref, width in zip(term, widths)]
    return jnp.concatenate([jnp.concatenate(reals, 1), jnp.concatenate(imags, 1)], 0)


def join_kernel(place, mine, theirs, high, low):
    chips, rows, _ = mine.shape
    for chip in range(chips):
        turn = lax.rem(place[0] - chip + chips, chips)
        one, other = mine[turn], theirs[turn]
        for core in (0, 1):
            block = jnp.where(place[1] == core, one, other)
            where = pl.ds((2 * chip + core) * rows, rows)
            high[where, :], low[where, :] = halves_of(block)


def joined(place, mine, theirs):
    chips, rows, columns = mine.shape
    return pl.pallas_call(
        join_kernel,
        in_specs=[pl.BlockSpec(memory_space=pltpu.SMEM)] + [pl.BlockSpec((chips, rows, columns), lambda: (0, 0, 0))] * 2,
        out_specs=[pl.BlockSpec(memory_space=pltpu.VMEM)] * 2,
        out_shape=[jax.ShapeDtypeStruct((2 * chips * rows, columns), jnp.bfloat16)] * 2,
        compiler_params=pltpu.CompilerParams(vmem_limit_bytes=12 * 1024 * 1024),
        cost_estimate=pl.CostEstimate(flops=0, bytes_accessed=0, transcendentals=0),
    )(place, mine, theirs)


def rows_kernel(tree, *refs):
    out = refs[-1]
    terms, matrices = jax.tree.unflatten(tree, refs[:-1])
    flat = whole_rows(terms[0])
    for term in terms[1:]:
        flat = flat + whole_rows(term)
    count = flat.shape[0] // 2
    high, low = halves_of(flat)
    both = jnp.concatenate([high, low], 0)
    for number, matrix in enumerate(matrices):
        first = 0
        for piece in matrix:
            product = dot(both, piece[0][...])
            product = product[: 2 * count] + product[2 * count :] + dot(high, piece[1][...])
            width = product.shape[1] // 2
            columns = slice(first, first + width)
            out[number, 0, :, columns] = product[:count, :width] - product[count:, width:]
            out[number, 1, :, columns] = product[:count, width:] + product[count:, :width]
            first += width


def rows_times(terms, matrices, count, bands):
    flat, tree = jax.tree.flatten((terms, matrices))
    in_vmem = pl.BlockSpec(memory_space=pltpu.VMEM)
    return pl.pallas_call(
        functools.partial(rows_kernel, tree),
        in_specs=[in_vmem if one.dtype == jnp.bfloat16 else pl.BlockSpec() for one in flat],
        out_shape=jax.ShapeDtypeStruct((len(matrices), 2, count, bands), jnp.float32),
        compiler_params=pltpu.CompilerParams(vmem_limit_bytes=12 * 1024 * 1024),
        cost_estimate=pl.CostEstimate(flops=0, bytes_accessed=0, transcendentals=0),
    )(*flat)


def packed(states, kpoint, first, width):
    return jnp.concatenate([s[kpoint, first : first + width] for s in states], 0)


def after(value, earlier):
    return lax.optimization_barrier((value, earlier))[0]


def other_core(block):
    size = lax.axis_size("pw")
    return lax.ppermute(block, "pw", [(i, i ^ 1) for i in range(size)])


def other_chip(block, distance):
    size = lax.axis_size("pw")
    return lax.ppermute(block, "pw", [(i, (i + 2 * distance) % size) for i in range(size)])


def sum_to_rows(mine, theirs):
    chips = mine.shape[0]
    chip = lax.axis_index("pw") // 2
    half = mine + other_core(theirs)

    def block(place):
        return lax.dynamic_index_in_dim(half, place % chips, 0, keepdims=False)

    received = [other_chip(block(chip + d), d) for d in range(1, chips)]
    return sum(received, block(chip))


def rows_to_core(rows):
    chips = lax.axis_size("pw") // 2
    return jnp.stack([rows] + [other_chip(rows, d) for d in range(1, chips)], 0)


def shards(states_re, states_im):
    kcount, bands, _ = states_re.shape
    ka_width = lax.axis_size("ka")
    pw_width = lax.axis_size("pw")
    band_rows = bands // pw_width
    ka_place = lax.axis_index("ka")
    first_band = lax.axis_index("pw") * band_rows
    core = (lax.axis_index("pw") % 2).reshape(1).astype(jnp.int32)
    place = jnp.stack([lax.axis_index("pw") // 2, lax.axis_index("pw") % 2]).astype(jnp.int32)
    quarter = bands // 4
    widths = [2 * quarter, quarter, quarter]
    firsts = [sum(widths[:i]) for i in range(len(widths))]
    to_previous = [(i, (i - 1) % ka_width) for i in range(ka_width)]
    blocks = [tuple(state[0, : widths[0]] for state in (states_re, states_im))]
    blocks += [packed((states_re, states_im), 0, first, width) for first, width in zip(firsts[1:], widths[1:])]

    def send(number, *earlier):
        return lax.ppermute(after(blocks[number], earlier) if earlier else blocks[number], "ka", to_previous)

    arrivals = [send(0)]
    states = after((states_re, states_im), blocks[0])
    last = kcount - 1
    terms = [margin_section(states, k) for k in range(last)]
    arrivals.append(send(1, terms))
    own_margins = [lax.psum(term, "pw") for term in terms]
    before = own_margins[0]
    for k in range(1, last):
        rows = jnp.stack([before[:, :bands], before[:, bands:]], 0)
        before = rows_times([[rows]], [[split(own_margins[k])]], bands, bands)[0]
        before = jnp.concatenate([before[0], before[1]], 1)
        own_margins[k] = before
    left = split(after(before, arrivals[0]))

    rows, span = [], []
    half = ready = None
    for number in range(len(widths)):
        piece = arrivals[number]
        final = number == len(widths) - 1
        if final:
            reals = [one[:, : one.shape[1] // 2] for one in rows]
            imags = [one[:, one.shape[1] // 2 :] for one in rows]
            ready = lax.ppermute(after(jnp.concatenate(reals + imags, 1), (piece, span)), "ka", [(0, 1)])
        if half is not None:
            piece = after(piece, half)
        mine, theirs = margin_section(states, last, [piece], left, core)
        if number == 0:
            arrivals.append(send(2, arrivals[0], mine))
        rows.append(sum_to_rows(mine, after(theirs, ready) if final else theirs))
        half = rows_to_core(rows[-1])
        if final:
            received = [ready, lax.ppermute(rows[-1], "ka", [(0, 1)])]
            half = after(half, received[-1])
        span.append(joined(place, half, other_core(half)))

    row_index = lax.broadcasted_iota(jnp.int32, (band_rows, bands), 0) + first_band
    col_index = lax.broadcasted_iota(jnp.int32, (band_rows, bands), 1)
    eye_real = jnp.where((row_index == col_index) & (ka_place == 0), 1.0, 0.0).astype(jnp.float32)
    starts = [[jnp.stack([eye_real, jnp.zeros_like(eye_real)], 0)], received]
    for number in range(1, ka_width - 1):
        line = rows_times(starts[-1:], [span], band_rows, bands)[0]
        starts.append([lax.ppermute(line, "ka", [(number, number + 1)])])

    margins = [[split(margin)] for margin in own_margins[:-1]] + [[left]]
    lines = rows_times(starts, margins + [span], band_rows, bands)
    return jnp.moveaxis(lines, 1, 2)


def solution(mesh):
    in_specs = (P("ka", None, "pw"), P("ka", None, "pw"))
    out_specs = P("ka", "pw", None, None)
    return jax.shard_map(shards, mesh=mesh, in_specs=in_specs, out_specs=out_specs, check_vma=False)
```

```python
import functools

import jax
import jax.numpy as jnp
from jax import lax
from jax.experimental import pallas as pl
from jax.experimental.pallas import tpu as pltpu
from jax.sharding import PartitionSpec as P

VMEM_LIMIT = 40 * 1024 * 1024


def halves_of(value):
    high = value.astype(jnp.bfloat16)
    return high, (value - high.astype(jnp.float32)).astype(jnp.bfloat16)


def dot(left, right, across=0):
    return lax.dot_general(left, right, (((1,), (across,)), ((), ())), preferred_element_type=jnp.float32)


def turned(value):
    width = value.shape[1] // 2
    return jnp.concatenate([-value[:, width:], value[:, :width]], 1)


def margin_kernel(steps, pieces, with_left, by_core, *refs):
    refs = list(refs)
    core = refs.pop(0) if by_core else None
    own_re, own_im = refs[:2]
    real_part = jnp.concatenate([ref[...] for ref in refs[2 : 2 + pieces]], 0)
    imag_part = jnp.concatenate([ref[...] for ref in refs[2 + pieces : 2 + 2 * pieces]], 0)
    refs = refs[2 + 2 * pieces :]
    left_high, left_low = refs[:2] if with_left else (None, None)
    outs, total = refs[2 if with_left else 0 : -1], refs[-1]
    step = pl.program_id(0)
    other = jnp.concatenate([jnp.concatenate([real_part, imag_part], 1), jnp.concatenate([imag_part, -real_part], 1)], 0)
    term = dot(jnp.concatenate([own_re[...], own_im[...]], 1), other, 1)

    @pl.when(step == 0)
    def _():
        total[...] = term

    @pl.when(step > 0)
    def _():
        total[...] += term

    @pl.when(step == steps - 1)
    def _():
        if with_left:
            bands = left_high.shape[0]
            value = total[...]
            product = jnp.zeros_like(value)
            for first, factor in ((0, value), (bands, turned(value))):
                high, low = halves_of(factor)
                columns = slice(first, first + bands)
                product += dot(left_high[:, columns], high)
                product += dot(left_high[:, columns], low)
                product += dot(left_low[:, columns], high)
            total[...] = product
        if by_core:
            mine, theirs = outs
            rows = mine.shape[1]
            for chip in range(mine.shape[0]):
                for out, which in ((mine, core[0]), (theirs, 1 - core[0])):
                    first = pl.multiple_of((2 * chip + which) * rows, rows)
                    out[chip] = total[pl.ds(first, rows), :]
        else:
            outs[0][...] = total[...]


def margin_section(states, kpoint, others=None, left=None, core=None):
    _, bands, waves = states[0].shape
    depth = min(1024, waves)
    steps = waves // depth
    own = pl.BlockSpec((None, bands, depth), lambda step: (kpoint, 0, step))
    if others is None:
        width = bands
        other_specs = [pl.BlockSpec((None, bands, depth), lambda step: (kpoint + 1, 0, step))] * 2
        others = states
    else:
        packs = [other if isinstance(other, tuple) else (other, other) for other in others]
        apart = [isinstance(other, tuple) for other in others]
        widths = [pack[0].shape[0] // (1 if one else 2) for pack, one in zip(packs, apart)]
        width = sum(widths)
        other_specs = [pl.BlockSpec((one, depth), lambda step: (0, step)) for one in widths]
        for one, alone in zip(widths, apart):
            other_specs.append(pl.BlockSpec((one, depth), functools.partial(lambda row, step: (row, step), 0 if alone else 1)))
        others = [pack[0] for pack in packs] + [pack[1] for pack in packs]
    operands, specs = [*states, *others], [own, own, *other_specs]
    if left is not None:
        operands += left
        specs += [pl.BlockSpec((bands, 2 * bands), lambda step: (0, 0))] * 2
    if core is not None:
        operands = [core, *operands]
        specs = [pl.BlockSpec(memory_space=pltpu.SMEM), *specs]
        chips = lax.axis_size("pw") // 2
        shape = (chips, bands // (2 * chips), 2 * width)
        out_shape = [jax.ShapeDtypeStruct(shape, jnp.float32)] * 2
        out_specs = [pl.BlockSpec(shape, lambda step: (0, 0, 0))] * 2
    else:
        out_shape = jax.ShapeDtypeStruct((bands, 2 * width), jnp.float32)
        out_specs = pl.BlockSpec((bands, 2 * width), lambda step: (0, 0))
    return pl.pallas_call(
        functools.partial(margin_kernel, steps, len(other_specs) // 2, left is not None, core is not None),
        grid=(steps,),
        in_specs=specs,
        out_specs=out_specs,
        out_shape=out_shape,
        scratch_shapes=[pltpu.VMEM((bands, 2 * width), jnp.float32)],
        compiler_params=pltpu.CompilerParams(vmem_limit_bytes=VMEM_LIMIT),
        cost_estimate=pl.CostEstimate(flops=0, bytes_accessed=0, transcendentals=0),
    )(*operands)


def split_kernel(value, high, low):
    high[...], low[...] = halves_of(value[...])


def split(value):
    return pl.pallas_call(
        split_kernel,
        out_shape=[jax.ShapeDtypeStruct(value.shape, jnp.bfloat16)] * 2,
        compiler_params=pltpu.CompilerParams(vmem_limit_bytes=VMEM_LIMIT),
    )(value)


def whole_rows(term):
    if len(term) == 1 and len(term[0].shape) == 3:
        rows = term[0][...]
        return jnp.concatenate([rows[0], rows[1]], 0)
    widths = [ref.shape[1] // 2 for ref in term]
    reals = [ref[:, :width] for ref, width in zip(term, widths)]
    imags = [ref[:, width:] for ref, width in zip(term, widths)]
    return jnp.concatenate([jnp.concatenate(reals, 1), jnp.concatenate(imags, 1)], 0)


def join_kernel(place, mine, theirs, high, low):
    chips, rows, _ = mine.shape
    for chip in range(chips):
        turn = lax.rem(place[0] - chip + chips, chips)
        one, other = mine[turn], theirs[turn]
        for core in (0, 1):
            block = jnp.where(place[1] == core, one, other)
            where = pl.ds((2 * chip + core) * rows, rows)
            high[where, :], low[where, :] = halves_of(block)


def joined(place, mine, theirs):
    chips, rows, columns = mine.shape
    return pl.pallas_call(
        join_kernel,
        in_specs=[pl.BlockSpec(memory_space=pltpu.SMEM)] + [pl.BlockSpec((chips, rows, columns), lambda: (0, 0, 0))] * 2,
        out_specs=[pl.BlockSpec(memory_space=pltpu.VMEM)] * 2,
        out_shape=[jax.ShapeDtypeStruct((2 * chips * rows, columns), jnp.bfloat16)] * 2,
        compiler_params=pltpu.CompilerParams(vmem_limit_bytes=12 * 1024 * 1024),
        cost_estimate=pl.CostEstimate(flops=0, bytes_accessed=0, transcendentals=0),
    )(place, mine, theirs)


def times_into(out, by_row, both, high, pieces):
    count = high.shape[0] // 2
    first = 0
    for piece_high, piece_low in pieces:
        product = dot(both, piece_high)
        product = product[: 2 * count] + product[2 * count :] + dot(high, piece_low)
        width = product.shape[1] // 2
        columns = slice(first, first + width)
        real_part = product[:count, :width] - product[count:, width:]
        imag_part = product[:count, width:] + product[count:, :width]
        if by_row:
            out[:, 0, columns] = real_part
            out[:, 1, columns] = imag_part
        else:
            out[0, :, columns] = real_part
            out[1, :, columns] = imag_part
        first += width


def rows_kernel(tree, fetched, *refs):
    if fetched:
        *refs, out, buffer, sems = refs
        refs, sources = refs[:-fetched], refs[-fetched:]
        copies = [pltpu.make_async_copy(source, buffer.at[i], sems.at[i]) for i, source in enumerate(sources)]
        for copy in copies:
            copy.start()
    else:
        *refs, out = refs
    terms, pieces = jax.tree.unflatten(tree, refs)
    flat = whole_rows(terms[0])
    for term in terms[1:]:
        flat = flat + whole_rows(term)
    high, low = halves_of(flat)
    both = jnp.concatenate([high, low], 0)
    times_into(out.at[fetched], fetched > 0, both, high, [(one[...], two[...]) for one, two in pieces])
    for i in range(fetched):
        copies[i].wait()
        times_into(out.at[i], True, both, high, [halves_of(buffer[i])])


def rows_times(terms, pieces, count, bands, fetched=()):
    flat, tree = jax.tree.flatten((terms, pieces))
    scratch = []
    if fetched:
        scratch = [pltpu.VMEM((len(fetched), bands, 2 * bands), jnp.float32), pltpu.SemaphoreType.DMA((len(fetched),))]
    return pl.pallas_call(
        functools.partial(rows_kernel, tree, len(fetched)),
        in_specs=[pl.BlockSpec()] * len(flat) + [pl.BlockSpec(memory_space=pl.ANY)] * len(fetched),
        out_shape=jax.ShapeDtypeStruct((len(fetched) + 1, *((count, 2) if fetched else (2, count)), bands), jnp.float32),
        scratch_shapes=scratch,
        compiler_params=pltpu.CompilerParams(vmem_limit_bytes=VMEM_LIMIT),
        cost_estimate=pl.CostEstimate(flops=0, bytes_accessed=0, transcendentals=0),
    )(*flat, *fetched)


def packed(states, kpoint, first, width):
    return jnp.concatenate([s[kpoint, first : first + width] for s in states], 0)


def after(value, earlier):
    return lax.optimization_barrier((value, earlier))[0]


def other_core(block):
    size = lax.axis_size("pw")
    return lax.ppermute(block, "pw", [(i, i ^ 1) for i in range(size)])


def other_chip(block, distance):
    size = lax.axis_size("pw")
    return lax.ppermute(block, "pw", [(i, (i + 2 * distance) % size) for i in range(size)])


def sum_to_rows(mine, theirs):
    chips = mine.shape[0]
    chip = lax.axis_index("pw") // 2
    half = mine + other_core(theirs)

    def block(place):
        return lax.dynamic_index_in_dim(half, place % chips, 0, keepdims=False)

    received = [other_chip(block(chip + d), d) for d in range(1, chips)]
    return sum(received, block(chip))


def rows_to_core(rows):
    chips = lax.axis_size("pw") // 2
    return jnp.stack([rows] + [other_chip(rows, d) for d in range(1, chips)], 0)


def shards(states_re, states_im):
    kcount, bands, _ = states_re.shape
    ka_width = lax.axis_size("ka")
    pw_width = lax.axis_size("pw")
    band_rows = bands // pw_width
    ka_place = lax.axis_index("ka")
    first_band = lax.axis_index("pw") * band_rows
    core = (lax.axis_index("pw") % 2).reshape(1).astype(jnp.int32)
    place = jnp.stack([lax.axis_index("pw") // 2, lax.axis_index("pw") % 2]).astype(jnp.int32)
    quarter = bands // 4
    widths = [2 * quarter, quarter, quarter]
    firsts = [sum(widths[:i]) for i in range(len(widths))]
    to_previous = [(i, (i - 1) % ka_width) for i in range(ka_width)]
    blocks = [tuple(state[0, : widths[0]] for state in (states_re, states_im))]
    blocks += [packed((states_re, states_im), 0, first, width) for first, width in zip(firsts[1:], widths[1:])]

    def send(number, *earlier):
        return lax.ppermute(after(blocks[number], earlier) if earlier else blocks[number], "ka", to_previous)

    arrivals = [send(0)]
    states = after((states_re, states_im), blocks[0])
    last = kcount - 1
    terms = [margin_section(states, k) for k in range(last)]
    arrivals.append(send(1, terms))
    own_margins = [lax.psum(term, "pw") for term in terms]
    before = own_margins[0]
    for k in range(1, last):
        rows = jnp.stack([before[:, :bands], before[:, bands:]], 0)
        before = rows_times([[rows]], [split(own_margins[k])], bands, bands)[0]
        before = jnp.concatenate([before[0], before[1]], 1)
        own_margins[k] = before
    left = split(after(before, arrivals[0]))

    rows, span = [], []
    half = ready = None
    for number in range(len(widths)):
        piece = arrivals[number]
        final = number == len(widths) - 1
        if final:
            reals = [one[:, : one.shape[1] // 2] for one in rows]
            imags = [one[:, one.shape[1] // 2 :] for one in rows]
            ready = lax.ppermute(after(jnp.concatenate(reals + imags, 1), (piece, span)), "ka", [(0, 1)])
        if half is not None:
            piece = after(piece, half)
        mine, theirs = margin_section(states, last, [piece], left, core)
        if number == 0:
            arrivals.append(send(2, arrivals[0], mine))
        rows.append(sum_to_rows(mine, after(theirs, ready) if final else theirs))
        half = rows_to_core(rows[-1])
        if final:
            received = [ready, lax.ppermute(rows[-1], "ka", [(0, 1)])]
            half = after(half, received[-1])
        span.append(joined(place, half, other_core(half)))

    row_index = lax.broadcasted_iota(jnp.int32, (band_rows, bands), 0) + first_band
    col_index = lax.broadcasted_iota(jnp.int32, (band_rows, bands), 1)
    eye_real = jnp.where((row_index == col_index) & (ka_place == 0), 1.0, 0.0).astype(jnp.float32)
    starts = [[jnp.stack([eye_real, jnp.zeros_like(eye_real)], 0)], received]
    for number in range(1, ka_width - 1):
        line = rows_times(starts[-1:], span, band_rows, bands)[0]
        starts.append([lax.ppermute(line, "ka", [(number, number + 1)])])

    return rows_times(starts, span, band_rows, bands, own_margins)


def solution(mesh):
    in_specs = (P("ka", None, "pw"), P("ka", None, "pw"))
    out_specs = P("ka", "pw", None, None)
    return jax.shard_map(shards, mesh=mesh, in_specs=in_specs, out_specs=out_specs, check_vma=False)
```

```python
import functools

import jax
import jax.numpy as jnp
from jax import lax
from jax.experimental import pallas as pl
from jax.experimental.pallas import tpu as pltpu
from jax.sharding import PartitionSpec as P

VMEM_LIMIT = 40 * 1024 * 1024


def halves_of(value):
    high = value.astype(jnp.bfloat16)
    return high, (value - high.astype(jnp.float32)).astype(jnp.bfloat16)


def dot(left, right, across=0):
    return lax.dot_general(left, right, (((1,), (across,)), ((), ())), preferred_element_type=jnp.float32)


def turned(value):
    width = value.shape[1] // 2
    return jnp.concatenate([-value[:, width:], value[:, :width]], 1)


def margin_kernel(steps, pieces, with_left, by_core, *refs):
    refs = list(refs)
    core = refs.pop(0) if by_core else None
    own_re, own_im = refs[:2]
    real_part = jnp.concatenate([ref[...] for ref in refs[2 : 2 + pieces]], 0)
    imag_part = jnp.concatenate([ref[...] for ref in refs[2 + pieces : 2 + 2 * pieces]], 0)
    refs = refs[2 + 2 * pieces :]
    left_high, left_low = refs[:2] if with_left else (None, None)
    outs, total = refs[2 if with_left else 0 : -1], refs[-1]
    step = pl.program_id(0)
    other = jnp.concatenate([jnp.concatenate([real_part, imag_part], 1), jnp.concatenate([imag_part, -real_part], 1)], 0)
    term = dot(jnp.concatenate([own_re[...], own_im[...]], 1), other, 1)

    @pl.when(step == 0)
    def _():
        total[...] = term

    @pl.when(step > 0)
    def _():
        total[...] += term

    @pl.when(step == steps - 1)
    def _():
        if with_left:
            bands = left_high.shape[0]
            value = total[...]
            product = jnp.zeros_like(value)
            for first, factor in ((0, value), (bands, turned(value))):
                high, low = halves_of(factor)
                columns = slice(first, first + bands)
                product += dot(left_high[:, columns], high)
                product += dot(left_high[:, columns], low)
                product += dot(left_low[:, columns], high)
            total[...] = product
        if by_core:
            mine, theirs = outs
            rows = mine.shape[1]
            for chip in range(mine.shape[0]):
                for out, which in ((mine, core[0]), (theirs, 1 - core[0])):
                    first = pl.multiple_of((2 * chip + which) * rows, rows)
                    out[chip] = total[pl.ds(first, rows), :]
        else:
            outs[0][...] = total[...]


def margin_section(states, kpoint, others=None, left=None, core=None):
    _, bands, waves = states[0].shape
    depth = min(1024, waves)
    steps = waves // depth
    own = pl.BlockSpec((None, bands, depth), lambda step: (kpoint, 0, step))
    if others is None:
        width = bands
        other_specs = [pl.BlockSpec((None, bands, depth), lambda step: (kpoint + 1, 0, step))] * 2
        others = states
    else:
        packs = [other if isinstance(other, tuple) else (other, other) for other in others]
        apart = [isinstance(other, tuple) for other in others]
        widths = [pack[0].shape[0] // (1 if one else 2) for pack, one in zip(packs, apart)]
        width = sum(widths)
        other_specs = [pl.BlockSpec((one, depth), lambda step: (0, step)) for one in widths]
        for one, alone in zip(widths, apart):
            other_specs.append(pl.BlockSpec((one, depth), functools.partial(lambda row, step: (row, step), 0 if alone else 1)))
        others = [pack[0] for pack in packs] + [pack[1] for pack in packs]
    operands, specs = [*states, *others], [own, own, *other_specs]
    if left is not None:
        operands += left
        specs += [pl.BlockSpec((bands, 2 * bands), lambda step: (0, 0))] * 2
    if core is not None:
        operands = [core, *operands]
        specs = [pl.BlockSpec(memory_space=pltpu.SMEM), *specs]
        chips = lax.axis_size("pw") // 2
        shape = (chips, bands // (2 * chips), 2 * width)
        out_shape = [jax.ShapeDtypeStruct(shape, jnp.float32)] * 2
        out_specs = [pl.BlockSpec(shape, lambda step: (0, 0, 0))] * 2
    else:
        out_shape = jax.ShapeDtypeStruct((bands, 2 * width), jnp.float32)
        out_specs = pl.BlockSpec((bands, 2 * width), lambda step: (0, 0))
    return pl.pallas_call(
        functools.partial(margin_kernel, steps, len(other_specs) // 2, left is not None, core is not None),
        grid=(steps,),
        in_specs=specs,
        out_specs=out_specs,
        out_shape=out_shape,
        scratch_shapes=[pltpu.VMEM((bands, 2 * width), jnp.float32)],
        compiler_params=pltpu.CompilerParams(vmem_limit_bytes=VMEM_LIMIT),
        cost_estimate=pl.CostEstimate(flops=0, bytes_accessed=0, transcendentals=0),
    )(*operands)


def split_kernel(value, high, low):
    high[...], low[...] = halves_of(value[...])


def split(value):
    return pl.pallas_call(
        split_kernel,
        out_shape=[jax.ShapeDtypeStruct(value.shape, jnp.bfloat16)] * 2,
        compiler_params=pltpu.CompilerParams(vmem_limit_bytes=VMEM_LIMIT),
    )(value)


def whole_rows(term):
    if len(term) == 1 and len(term[0].shape) == 3:
        rows = term[0][...]
        return jnp.concatenate([rows[0], rows[1]], 0)
    widths = [ref.shape[1] // 2 for ref in term]
    reals = [ref[:, :width] for ref, width in zip(term, widths)]
    imags = [ref[:, width:] for ref, width in zip(term, widths)]
    return jnp.concatenate([jnp.concatenate(reals, 1), jnp.concatenate(imags, 1)], 0)


def join_kernel(place, *refs):
    *refs, out = refs
    pairs = len(refs) // 2
    total, first = out.shape[1] // 2, 0
    for mine, theirs in zip(refs[:pairs], refs[pairs:]):
        chips, rows, width = mine.shape
        for chip in range(chips):
            turn = lax.rem(place[0] - chip + chips, chips)
            one, other = mine[turn], theirs[turn]
            for core in (0, 1):
                high, low = halves_of(jnp.where(place[1] == core, one, other))
                where = slice((2 * chip + core) * rows, (2 * chip + core + 1) * rows)
                out[where, first : first + width] = high
                out[where, total + first : total + first + width] = low
        first += width


def joined(place, mine, theirs):
    chips, rows, _ = mine[0].shape
    columns = sum(one.shape[2] for one in mine)
    return pl.pallas_call(
        join_kernel,
        in_specs=[pl.BlockSpec(memory_space=pltpu.SMEM)] + [pl.BlockSpec()] * (2 * len(mine)),
        out_specs=pl.BlockSpec(memory_space=pltpu.VMEM),
        out_shape=jax.ShapeDtypeStruct((2 * chips * rows, 2 * columns), jnp.bfloat16),
        compiler_params=pltpu.CompilerParams(vmem_limit_bytes=VMEM_LIMIT),
        cost_estimate=pl.CostEstimate(flops=0, bytes_accessed=0, transcendentals=0),
    )(place, *mine, *theirs)


def times_into(out, by_row, both, high, pieces):
    count = high.shape[0] // 2
    first = 0
    for piece_high, piece_low in pieces:
        product = dot(both, piece_high)
        product = product[: 2 * count] + product[2 * count :] + dot(high, piece_low)
        width = product.shape[1] // 2
        columns = slice(first, first + width)
        real_part = product[:count, :width] - product[count:, width:]
        imag_part = product[:count, width:] + product[count:, :width]
        if by_row:
            out[:, 0, columns] = real_part
            out[:, 1, columns] = imag_part
        else:
            out[0, :, columns] = real_part
            out[1, :, columns] = imag_part
        first += width


def span_pieces(span, widths):
    total, first = span.shape[1] // 2, 0
    for width in widths:
        yield span[:, first : first + 2 * width], span[:, total + first : total + first + 2 * width]
        first += 2 * width


def split_rows(flat):
    high, low = halves_of(flat)
    return jnp.concatenate([high, low], 0), high


def hop_kernel(widths, *refs):
    *term, before, span, line, after_rows = refs
    flat = whole_rows(term)
    count = flat.shape[0] // 2
    times_into(line, False, *split_rows(flat), span_pieces(span, widths))
    after_rows[0] = before[0] + flat[:count]
    after_rows[1] = before[1] + flat[count:]


def hop(term, before, span, widths):
    return pl.pallas_call(
        functools.partial(hop_kernel, widths),
        out_shape=[jax.ShapeDtypeStruct(before.shape, jnp.float32)] * 2,
        compiler_params=pltpu.CompilerParams(vmem_limit_bytes=VMEM_LIMIT),
        cost_estimate=pl.CostEstimate(flops=0, bytes_accessed=0, transcendentals=0),
    )(*term, before, span)


def last_kernel(widths, fetched, *refs):
    *refs, out, buffer, sems = refs
    refs, sources = refs[:-fetched], refs[-fetched:]
    copies = [pltpu.make_async_copy(source, buffer.at[i], sems.at[i]) for i, source in enumerate(sources)]
    for copy in copies:
        copy.start()
    *terms, span = refs
    flat = whole_rows(terms[:1])
    for term in terms[1:]:
        flat = flat + whole_rows([term])
    both, high = split_rows(flat)
    times_into(out.at[fetched], True, both, high, span_pieces(span, widths))
    for i in range(fetched):
        copies[i].wait()
        times_into(out.at[i], True, both, high, [halves_of(buffer[i])])


def last_lines(terms, span, widths, fetched):
    _, count, bands = terms[0].shape
    return pl.pallas_call(
        functools.partial(last_kernel, widths, len(fetched)),
        in_specs=[pl.BlockSpec()] * (len(terms) + 1) + [pl.BlockSpec(memory_space=pl.ANY)] * len(fetched),
        out_shape=jax.ShapeDtypeStruct((len(fetched) + 1, count, 2, bands), jnp.float32),
        scratch_shapes=[
            pltpu.VMEM((len(fetched), bands, 2 * bands), jnp.float32),
            pltpu.SemaphoreType.DMA((len(fetched),)),
        ],
        compiler_params=pltpu.CompilerParams(vmem_limit_bytes=VMEM_LIMIT),
        cost_estimate=pl.CostEstimate(flops=0, bytes_accessed=0, transcendentals=0),
    )(*terms, span, *fetched)


def complex_dot(left, right):
    bands = left.shape[0]
    dots = [jnp.dot(left[:, i : i + bands], right, precision=lax.Precision.HIGH) for i in (0, bands)]
    return jnp.concatenate(
        [dots[0][:, :bands] - dots[1][:, bands:], dots[0][:, bands:] + dots[1][:, :bands]], 1
    )


def packed(states, kpoint, first, width):
    return jnp.concatenate([s[kpoint, first : first + width] for s in states], 0)


def after(value, earlier):
    return lax.optimization_barrier((value, earlier))[0]


def other_core(block):
    size = lax.axis_size("pw")
    return lax.ppermute(block, "pw", [(i, i ^ 1) for i in range(size)])


def other_chip(block, distance):
    size = lax.axis_size("pw")
    return lax.ppermute(block, "pw", [(i, (i + 2 * distance) % size) for i in range(size)])


def sum_to_rows(mine, theirs):
    chips = mine.shape[0]
    chip = lax.axis_index("pw") // 2
    half = mine + other_core(theirs)

    def block(place):
        return lax.dynamic_index_in_dim(half, place % chips, 0, keepdims=False)

    received = [other_chip(block(chip + d), d) for d in range(1, chips)]
    return sum(received, block(chip))


def rows_to_core(rows):
    chips = lax.axis_size("pw") // 2
    return jnp.stack([rows] + [other_chip(rows, d) for d in range(1, chips)], 0)


def shards(states_re, states_im):
    kcount, bands, _ = states_re.shape
    ka_width = lax.axis_size("ka")
    pw_width = lax.axis_size("pw")
    band_rows = bands // pw_width
    ka_place = lax.axis_index("ka")
    first_band = lax.axis_index("pw") * band_rows
    core = (lax.axis_index("pw") % 2).reshape(1).astype(jnp.int32)
    place = jnp.stack([lax.axis_index("pw") // 2, lax.axis_index("pw") % 2]).astype(jnp.int32)
    quarter = bands // 4
    widths = [2 * quarter, quarter, quarter]
    firsts = [sum(widths[:i]) for i in range(len(widths))]
    to_previous = [(i, (i - 1) % ka_width) for i in range(ka_width)]
    blocks = [tuple(state[0, : widths[0]] for state in (states_re, states_im))]
    blocks += [packed((states_re, states_im), 0, first, width) for first, width in zip(firsts[1:], widths[1:])]

    def send(number, *earlier):
        return lax.ppermute(after(blocks[number], earlier) if earlier else blocks[number], "ka", to_previous)

    arrivals = [send(0)]
    states = after((states_re, states_im), blocks[0])
    last = kcount - 1
    terms = [margin_section(states, k) for k in range(last)]
    arrivals.append(send(1, terms))
    own_margins = [lax.psum(term, "pw") for term in terms]
    before = own_margins[0]
    for k in range(1, last):
        before = own_margins[k] = complex_dot(before, own_margins[k])
    left = split(after(before, arrivals[0]))

    rows, halves, swapped = [], [], []
    ready = None
    for number in range(len(widths)):
        piece = arrivals[number]
        final = number == len(widths) - 1
        if final:
            reals = [one[:, : one.shape[1] // 2] for one in rows]
            imags = [one[:, one.shape[1] // 2 :] for one in rows]
            ready = lax.ppermute(after(jnp.concatenate(reals + imags, 1), (piece, swapped)), "ka", [(0, 1)])
        if halves:
            piece = after(piece, halves[-1])
        mine, theirs = margin_section(states, last, [piece], left, core)
        if number == 0:
            arrivals.append(send(2, arrivals[0], mine))
        rows.append(sum_to_rows(mine, after(theirs, ready) if final else theirs))
        half = rows_to_core(rows[-1])
        if final:
            received = [ready, lax.ppermute(rows[-1], "ka", [(0, 1)])]
            half = after(half, received[-1])
        halves.append(half)
        swapped.append(other_core(half))
    span = joined(place, halves, swapped)

    row_index = lax.broadcasted_iota(jnp.int32, (band_rows, bands), 0) + first_band
    col_index = lax.broadcasted_iota(jnp.int32, (band_rows, bands), 1)
    eye_real = jnp.where((row_index == col_index) & (ka_place == 0), 1.0, 0.0).astype(jnp.float32)
    start = jnp.stack([eye_real, jnp.zeros_like(eye_real)], 0)
    for number in range(1, ka_width - 1):
        line, start = hop(received, start, span, widths)
        received = [lax.ppermute(line, "ka", [(number, number + 1)])]

    return last_lines([start, *received], span, widths, own_margins)


def solution(mesh):
    in_specs = (P("ka", None, "pw"), P("ka", None, "pw"))
    out_specs = P("ka", "pw", None, None)
    return jax.shard_map(shards, mesh=mesh, in_specs=in_specs, out_specs=out_specs, check_vma=False)
```

```python
import functools

import jax
import jax.numpy as jnp
from jax import lax
from jax.experimental import pallas as pl
from jax.experimental.pallas import tpu as pltpu
from jax.sharding import PartitionSpec as P

VMEM_LIMIT = 40 * 1024 * 1024


def halves_of(value):
    high = value.astype(jnp.bfloat16)
    return high, (value - high.astype(jnp.float32)).astype(jnp.bfloat16)


def dot(left, right, across=0):
    return lax.dot_general(left, right, (((1,), (across,)), ((), ())), preferred_element_type=jnp.float32)


def turned(value):
    width = value.shape[1] // 2
    return jnp.concatenate([-value[:, width:], value[:, :width]], 1)


def margin_kernel(steps, pieces, with_left, by_core, *refs):
    refs = list(refs)
    core = refs.pop(0) if by_core else None
    own_re, own_im = refs[:2]
    real_part = jnp.concatenate([ref[...] for ref in refs[2 : 2 + pieces]], 0)
    imag_part = jnp.concatenate([ref[...] for ref in refs[2 + pieces : 2 + 2 * pieces]], 0)
    refs = refs[2 + 2 * pieces :]
    left_high, left_low = refs[:2] if with_left else (None, None)
    outs, total = refs[2 if with_left else 0 : -1], refs[-1]
    step = pl.program_id(0)
    other = jnp.concatenate([jnp.concatenate([real_part, imag_part], 1), jnp.concatenate([imag_part, -real_part], 1)], 0)
    term = dot(jnp.concatenate([own_re[...], own_im[...]], 1), other, 1)

    @pl.when(step == 0)
    def _():
        total[...] = term

    @pl.when(step > 0)
    def _():
        total[...] += term

    @pl.when(step == steps - 1)
    def _():
        if with_left:
            bands = left_high.shape[0]
            value = total[...]
            product = jnp.zeros_like(value)
            for first, factor in ((0, value), (bands, turned(value))):
                high, low = halves_of(factor)
                columns = slice(first, first + bands)
                product += dot(left_high[:, columns], high)
                product += dot(left_high[:, columns], low)
                product += dot(left_low[:, columns], high)
            total[...] = product
        if by_core:
            mine, theirs = outs
            rows = mine.shape[1]
            for chip in range(mine.shape[0]):
                for out, which in ((mine, core[0]), (theirs, 1 - core[0])):
                    first = pl.multiple_of((2 * chip + which) * rows, rows)
                    out[chip] = total[pl.ds(first, rows), :]
        else:
            outs[0][...] = total[...]


def margin_section(states, kpoint, others=None, left=None, core=None):
    _, bands, waves = states[0].shape
    depth = min(1024, waves)
    steps = waves // depth
    own = pl.BlockSpec((None, bands, depth), lambda step: (kpoint, 0, step))
    if others is None:
        width = bands
        other_specs = [pl.BlockSpec((None, bands, depth), lambda step: (kpoint + 1, 0, step))] * 2
        others = states
    else:
        packs = [other if isinstance(other, tuple) else (other, other) for other in others]
        apart = [isinstance(other, tuple) for other in others]
        widths = [pack[0].shape[0] // (1 if one else 2) for pack, one in zip(packs, apart)]
        width = sum(widths)
        other_specs = [pl.BlockSpec((one, depth), lambda step: (0, step)) for one in widths]
        for one, alone in zip(widths, apart):
            other_specs.append(pl.BlockSpec((one, depth), functools.partial(lambda row, step: (row, step), 0 if alone else 1)))
        others = [pack[0] for pack in packs] + [pack[1] for pack in packs]
    operands, specs = [*states, *others], [own, own, *other_specs]
    if left is not None:
        operands += left
        specs += [pl.BlockSpec((bands, 2 * bands), lambda step: (0, 0))] * 2
    if core is not None:
        operands = [core, *operands]
        specs = [pl.BlockSpec(memory_space=pltpu.SMEM), *specs]
        chips = lax.axis_size("pw") // 2
        shape = (chips, bands // (2 * chips), 2 * width)
        out_shape = [jax.ShapeDtypeStruct(shape, jnp.float32)] * 2
        out_specs = [pl.BlockSpec(shape, lambda step: (0, 0, 0))] * 2
    else:
        out_shape = jax.ShapeDtypeStruct((bands, 2 * width), jnp.float32)
        out_specs = pl.BlockSpec((bands, 2 * width), lambda step: (0, 0))
    return pl.pallas_call(
        functools.partial(margin_kernel, steps, len(other_specs) // 2, left is not None, core is not None),
        grid=(steps,),
        in_specs=specs,
        out_specs=out_specs,
        out_shape=out_shape,
        scratch_shapes=[pltpu.VMEM((bands, 2 * width), jnp.float32)],
        compiler_params=pltpu.CompilerParams(vmem_limit_bytes=VMEM_LIMIT),
        cost_estimate=pl.CostEstimate(flops=0, bytes_accessed=0, transcendentals=0),
    )(*operands)


def split_kernel(value, high, low):
    high[...], low[...] = halves_of(value[...])


def split(value):
    return pl.pallas_call(
        split_kernel,
        out_shape=[jax.ShapeDtypeStruct(value.shape, jnp.bfloat16)] * 2,
        compiler_params=pltpu.CompilerParams(vmem_limit_bytes=VMEM_LIMIT),
    )(value)


def whole_rows(term):
    if len(term) == 1 and len(term[0].shape) == 3:
        rows = term[0][...]
        return jnp.concatenate([rows[0], rows[1]], 0)
    widths = [ref.shape[1] // 2 for ref in term]
    reals = [ref[:, :width] for ref, width in zip(term, widths)]
    imags = [ref[:, width:] for ref, width in zip(term, widths)]
    return jnp.concatenate([jnp.concatenate(reals, 1), jnp.concatenate(imags, 1)], 0)


def join_kernel(place, *refs):
    *refs, out = refs
    pairs = len(refs) // 2
    total, first = out.shape[1] // 2, 0
    for number, (mine, theirs) in enumerate(zip(refs[:pairs], refs[pairs:])):
        chips, rows, width = mine.shape
        for chip in range(chips):
            turn = chip if number == pairs - 1 else lax.rem(place[0] - chip + chips, chips)
            one, other = mine[turn], theirs[turn]
            for core in (0, 1):
                high, low = halves_of(jnp.where(place[1] == core, one, other))
                where = slice((2 * chip + core) * rows, (2 * chip + core + 1) * rows)
                out[where, first : first + width] = high
                out[where, total + first : total + first + width] = low
        first += width


def joined(place, mine, theirs):
    chips, rows, _ = mine[0].shape
    columns = sum(one.shape[2] for one in mine)
    return pl.pallas_call(
        join_kernel,
        in_specs=[pl.BlockSpec(memory_space=pltpu.SMEM)] + [pl.BlockSpec()] * (2 * len(mine)),
        out_specs=pl.BlockSpec(memory_space=pltpu.VMEM),
        out_shape=jax.ShapeDtypeStruct((2 * chips * rows, 2 * columns), jnp.bfloat16),
        compiler_params=pltpu.CompilerParams(vmem_limit_bytes=VMEM_LIMIT),
        cost_estimate=pl.CostEstimate(flops=0, bytes_accessed=0, transcendentals=0),
    )(place, *mine, *theirs)


def times_into(out, by_row, both, high, pieces):
    count = high.shape[0] // 2
    first = 0
    for piece_high, piece_low in pieces:
        product = dot(both, piece_high)
        product = product[: 2 * count] + product[2 * count :] + dot(high, piece_low)
        width = product.shape[1] // 2
        columns = slice(first, first + width)
        real_part = product[:count, :width] - product[count:, width:]
        imag_part = product[:count, width:] + product[count:, :width]
        if by_row:
            out[:, 0, columns] = real_part
            out[:, 1, columns] = imag_part
        else:
            out[0, :, columns] = real_part
            out[1, :, columns] = imag_part
        first += width


def span_pieces(span, widths):
    total, first = span.shape[1] // 2, 0
    for width in widths:
        yield span[:, first : first + 2 * width], span[:, total + first : total + first + 2 * width]
        first += 2 * width


def split_rows(flat):
    high, low = halves_of(flat)
    return jnp.concatenate([high, low], 0), high


def hop_kernel(widths, *refs):
    *term, before, span, line, after_rows = refs
    flat = whole_rows(term)
    count = flat.shape[0] // 2
    times_into(line, False, *split_rows(flat), span_pieces(span, widths))
    after_rows[0] = before[0] + flat[:count]
    after_rows[1] = before[1] + flat[count:]


def hop(term, before, span, widths):
    return pl.pallas_call(
        functools.partial(hop_kernel, widths),
        out_shape=[jax.ShapeDtypeStruct(before.shape, jnp.float32)] * 2,
        compiler_params=pltpu.CompilerParams(vmem_limit_bytes=VMEM_LIMIT),
        cost_estimate=pl.CostEstimate(flops=0, bytes_accessed=0, transcendentals=0),
    )(*term, before, span)


def last_kernel(widths, fetched, *refs):
    *refs, out, buffer, sems = refs
    refs, sources = refs[:-fetched], refs[-fetched:]
    copies = [pltpu.make_async_copy(source, buffer.at[i], sems.at[i]) for i, source in enumerate(sources)]
    for copy in copies:
        copy.start()
    *terms, span = refs
    flat = whole_rows(terms[:1])
    for term in terms[1:]:
        flat = flat + whole_rows([term])
    both, high = split_rows(flat)
    times_into(out.at[fetched], True, both, high, span_pieces(span, widths))
    for i in range(fetched):
        copies[i].wait()
        times_into(out.at[i], True, both, high, [halves_of(buffer[i])])


def last_lines(terms, span, widths, fetched):
    _, count, bands = terms[0].shape
    return pl.pallas_call(
        functools.partial(last_kernel, widths, len(fetched)),
        in_specs=[pl.BlockSpec()] * (len(terms) + 1) + [pl.BlockSpec(memory_space=pl.ANY)] * len(fetched),
        out_shape=jax.ShapeDtypeStruct((len(fetched) + 1, count, 2, bands), jnp.float32),
        scratch_shapes=[
            pltpu.VMEM((len(fetched), bands, 2 * bands), jnp.float32),
            pltpu.SemaphoreType.DMA((len(fetched),)),
        ],
        compiler_params=pltpu.CompilerParams(vmem_limit_bytes=VMEM_LIMIT),
        cost_estimate=pl.CostEstimate(flops=0, bytes_accessed=0, transcendentals=0),
    )(*terms, span, *fetched)


def complex_dot(left, right):
    bands = left.shape[0]
    dots = [jnp.dot(left[:, i : i + bands], right, precision=lax.Precision.HIGH) for i in (0, bands)]
    return jnp.concatenate(
        [dots[0][:, :bands] - dots[1][:, bands:], dots[0][:, bands:] + dots[1][:, :bands]], 1
    )


def packed(states, kpoint, first, width):
    return jnp.concatenate([s[kpoint, first : first + width] for s in states], 0)


def after(value, earlier):
    return lax.optimization_barrier((value, earlier))[0]


def other_core(block):
    size = lax.axis_size("pw")
    return lax.ppermute(block, "pw", [(i, i ^ 1) for i in range(size)])


def other_chip(block, distance):
    size = lax.axis_size("pw")
    return lax.ppermute(block, "pw", [(i, (i + 2 * distance) % size) for i in range(size)])


def sum_to_rows(mine, theirs):
    chips = mine.shape[0]
    chip = lax.axis_index("pw") // 2
    half = mine + other_core(theirs)

    def block(place):
        return lax.dynamic_index_in_dim(half, place % chips, 0, keepdims=False)

    received = [other_chip(block(chip + d), d) for d in range(1, chips)]
    return sum(received, block(chip))


def across_chips(blocks):
    size = lax.axis_size("pw")
    groups = [list(range(core, size, 2)) for core in (0, 1)]
    return lax.all_to_all(blocks, "pw", 0, 0, axis_index_groups=groups, tiled=True)


def rows_to_core(rows):
    chips = lax.axis_size("pw") // 2
    return jnp.stack([rows] + [other_chip(rows, d) for d in range(1, chips)], 0)


def shards(states_re, states_im):
    kcount, bands, _ = states_re.shape
    ka_width = lax.axis_size("ka")
    pw_width = lax.axis_size("pw")
    band_rows = bands // pw_width
    ka_place = lax.axis_index("ka")
    first_band = lax.axis_index("pw") * band_rows
    core = (lax.axis_index("pw") % 2).reshape(1).astype(jnp.int32)
    place = jnp.stack([lax.axis_index("pw") // 2, lax.axis_index("pw") % 2]).astype(jnp.int32)
    quarter = bands // 4
    widths = [2 * quarter, quarter, quarter]
    firsts = [sum(widths[:i]) for i in range(len(widths))]
    to_previous = [(i, (i - 1) % ka_width) for i in range(ka_width)]
    blocks = [tuple(state[0, : widths[0]] for state in (states_re, states_im))]
    blocks += [packed((states_re, states_im), 0, first, width) for first, width in zip(firsts[1:], widths[1:])]

    def send(number, *earlier):
        return lax.ppermute(after(blocks[number], earlier) if earlier else blocks[number], "ka", to_previous)

    arrivals = [send(0)]
    states = after((states_re, states_im), blocks[0])
    last = kcount - 1
    terms = [margin_section(states, k) for k in range(last)]
    arrivals.append(send(1, terms))
    own_margins = [lax.psum(term, "pw") for term in terms]
    before = own_margins[0]
    for k in range(1, last):
        before = own_margins[k] = complex_dot(before, own_margins[k])
    left = split(after(before, arrivals[0]))

    rows, halves, swapped = [], [], []
    ready = None
    for number in range(len(widths)):
        piece = arrivals[number]
        final = number == len(widths) - 1
        if final:
            reals = [one[:, : one.shape[1] // 2] for one in rows]
            imags = [one[:, one.shape[1] // 2 :] for one in rows]
            ready = lax.ppermute(after(jnp.concatenate(reals + imags, 1), (piece, swapped)), "ka", [(0, 1)])
        if halves:
            piece = after(piece, halves[-1])
        mine, theirs = margin_section(states, last, [piece], left, core)
        if number == 0:
            arrivals.append(send(2, arrivals[0], mine))
        if final:
            rows.append(jnp.sum(across_chips(mine + other_core(after(theirs, ready))), 0))
            half = across_chips(jnp.broadcast_to(rows[-1], mine.shape))
        else:
            rows.append(sum_to_rows(mine, theirs))
            half = rows_to_core(rows[-1])
        if final:
            received = [ready, lax.ppermute(rows[-1], "ka", [(0, 1)])]
            half = after(half, received[-1])
        halves.append(half)
        swapped.append(other_core(half))
    span = joined(place, halves, swapped)

    row_index = lax.broadcasted_iota(jnp.int32, (band_rows, bands), 0) + first_band
    col_index = lax.broadcasted_iota(jnp.int32, (band_rows, bands), 1)
    eye_real = jnp.where((row_index == col_index) & (ka_place == 0), 1.0, 0.0).astype(jnp.float32)
    start = jnp.stack([eye_real, jnp.zeros_like(eye_real)], 0)
    for number in range(1, ka_width - 1):
        line, start = hop(received, start, span, widths)
        received = [lax.ppermute(line, "ka", [(number, number + 1)])]

    return last_lines([start, *received], span, widths, own_margins)


def solution(mesh):
    in_specs = (P("ka", None, "pw"), P("ka", None, "pw"))
    out_specs = P("ka", "pw", None, None)
    return jax.shard_map(shards, mesh=mesh, in_specs=in_specs, out_specs=out_specs, check_vma=False)
```

```python
import functools

import jax
import jax.numpy as jnp
from jax import lax
from jax.experimental import pallas as pl
from jax.experimental.pallas import tpu as pltpu
from jax.sharding import PartitionSpec as P

VMEM_LIMIT = 40 * 1024 * 1024


def halves_of(value):
    high = value.astype(jnp.bfloat16)
    return high, (value - high.astype(jnp.float32)).astype(jnp.bfloat16)


def dot(left, right, across=0):
    return lax.dot_general(left, right, (((1,), (across,)), ((), ())), preferred_element_type=jnp.float32)


def turned(value):
    width = value.shape[1] // 2
    return jnp.concatenate([-value[:, width:], value[:, :width]], 1)


def margin_kernel(steps, pieces, with_left, by_core, *refs):
    refs = list(refs)
    core = refs.pop(0) if by_core else None
    own_re, own_im = refs[:2]
    real_part = jnp.concatenate([ref[...] for ref in refs[2 : 2 + pieces]], 0)
    imag_part = jnp.concatenate([ref[...] for ref in refs[2 + pieces : 2 + 2 * pieces]], 0)
    refs = refs[2 + 2 * pieces :]
    left_high, left_low = refs[:2] if with_left else (None, None)
    outs, total = refs[2 if with_left else 0 : -1], refs[-1]
    step = pl.program_id(0)
    other = jnp.concatenate([jnp.concatenate([real_part, imag_part], 1), jnp.concatenate([imag_part, -real_part], 1)], 0)
    term = dot(jnp.concatenate([own_re[...], own_im[...]], 1), other, 1)

    @pl.when(step == 0)
    def _():
        total[...] = term

    @pl.when(step > 0)
    def _():
        total[...] += term

    @pl.when(step == steps - 1)
    def _():
        if with_left:
            bands = left_high.shape[0]
            value = total[...]
            product = jnp.zeros_like(value)
            for first, factor in ((0, value), (bands, turned(value))):
                high, low = halves_of(factor)
                columns = slice(first, first + bands)
                product += dot(left_high[:, columns], high)
                product += dot(left_high[:, columns], low)
                product += dot(left_low[:, columns], high)
            total[...] = product
        if by_core:
            mine, theirs = outs
            rows = mine.shape[1]
            for chip in range(mine.shape[0]):
                for out, which in ((mine, core[0]), (theirs, 1 - core[0])):
                    first = pl.multiple_of((2 * chip + which) * rows, rows)
                    out[chip] = total[pl.ds(first, rows), :]
        else:
            outs[0][...] = total[...]


def margin_section(states, kpoint, others=None, left=None, core=None):
    _, bands, waves = states[0].shape
    depth = min(1024, waves)
    steps = waves // depth
    own = pl.BlockSpec((None, bands, depth), lambda step: (kpoint, 0, step))
    if others is None:
        width = bands
        other_specs = [pl.BlockSpec((None, bands, depth), lambda step: (kpoint + 1, 0, step))] * 2
        others = states
    else:
        packs = [other if isinstance(other, tuple) else (other, other) for other in others]
        apart = [isinstance(other, tuple) for other in others]
        widths = [pack[0].shape[0] // (1 if one else 2) for pack, one in zip(packs, apart)]
        width = sum(widths)
        other_specs = [pl.BlockSpec((one, depth), lambda step: (0, step)) for one in widths]
        for one, alone in zip(widths, apart):
            other_specs.append(pl.BlockSpec((one, depth), functools.partial(lambda row, step: (row, step), 0 if alone else 1)))
        others = [pack[0] for pack in packs] + [pack[1] for pack in packs]
    operands, specs = [*states, *others], [own, own, *other_specs]
    if left is not None:
        operands += left
        specs += [pl.BlockSpec((bands, 2 * bands), lambda step: (0, 0))] * 2
    if core is not None:
        operands = [core, *operands]
        specs = [pl.BlockSpec(memory_space=pltpu.SMEM), *specs]
        chips = lax.axis_size("pw") // 2
        shape = (chips, bands // (2 * chips), 2 * width)
        out_shape = [jax.ShapeDtypeStruct(shape, jnp.float32)] * 2
        out_specs = [pl.BlockSpec(shape, lambda step: (0, 0, 0))] * 2
    else:
        out_shape = jax.ShapeDtypeStruct((bands, 2 * width), jnp.float32)
        out_specs = pl.BlockSpec((bands, 2 * width), lambda step: (0, 0))
    return pl.pallas_call(
        functools.partial(margin_kernel, steps, len(other_specs) // 2, left is not None, core is not None),
        grid=(steps,),
        in_specs=specs,
        out_specs=out_specs,
        out_shape=out_shape,
        scratch_shapes=[pltpu.VMEM((bands, 2 * width), jnp.float32)],
        compiler_params=pltpu.CompilerParams(vmem_limit_bytes=VMEM_LIMIT),
        cost_estimate=pl.CostEstimate(flops=0, bytes_accessed=0, transcendentals=0),
    )(*operands)


def split_kernel(value, high, low):
    high[...], low[...] = halves_of(value[...])


def split(value):
    return pl.pallas_call(
        split_kernel,
        out_shape=[jax.ShapeDtypeStruct(value.shape, jnp.bfloat16)] * 2,
        compiler_params=pltpu.CompilerParams(vmem_limit_bytes=VMEM_LIMIT),
    )(value)


def whole_rows(term):
    if len(term) == 1 and len(term[0].shape) == 3:
        rows = term[0][...]
        return jnp.concatenate([rows[0], rows[1]], 0)
    widths = [ref.shape[1] // 2 for ref in term]
    reals = [ref[:, :width] for ref, width in zip(term, widths)]
    imags = [ref[:, width:] for ref, width in zip(term, widths)]
    return jnp.concatenate([jnp.concatenate(reals, 1), jnp.concatenate(imags, 1)], 0)


def join_kernel(place, *refs):
    *refs, out = refs
    pairs = len(refs) // 2
    total, first = out.shape[1] // 2, 0
    for mine, theirs in zip(refs[:pairs], refs[pairs:]):
        chips, rows, width = mine.shape
        for chip in range(chips):
            turn = lax.rem(place[0] - chip + chips, chips)
            one, other = mine[turn], theirs[turn]
            for core in (0, 1):
                high, low = halves_of(jnp.where(place[1] == core, one, other))
                where = slice((2 * chip + core) * rows, (2 * chip + core + 1) * rows)
                out[where, first : first + width] = high
                out[where, total + first : total + first + width] = low
        first += width


def joined(place, mine, theirs):
    chips, rows, _ = mine[0].shape
    columns = sum(one.shape[2] for one in mine)
    return pl.pallas_call(
        join_kernel,
        in_specs=[pl.BlockSpec(memory_space=pltpu.SMEM)] + [pl.BlockSpec()] * (2 * len(mine)),
        out_specs=pl.BlockSpec(memory_space=pltpu.VMEM),
        out_shape=jax.ShapeDtypeStruct((2 * chips * rows, 2 * columns), jnp.bfloat16),
        compiler_params=pltpu.CompilerParams(vmem_limit_bytes=VMEM_LIMIT),
        cost_estimate=pl.CostEstimate(flops=0, bytes_accessed=0, transcendentals=0),
    )(place, *mine, *theirs)


def times_into(out, by_row, both, high, pieces):
    count = high.shape[0] // 2
    first = 0
    for piece_high, piece_low in pieces:
        product = dot(both, piece_high)
        product = product[: 2 * count] + product[2 * count :] + dot(high, piece_low)
        width = product.shape[1] // 2
        columns = slice(first, first + width)
        real_part = product[:count, :width] - product[count:, width:]
        imag_part = product[:count, width:] + product[count:, :width]
        if by_row:
            out[:, 0, columns] = real_part
            out[:, 1, columns] = imag_part
        else:
            out[0, :, columns] = real_part
            out[1, :, columns] = imag_part
        first += width


def span_pieces(span, widths):
    total, first = span.shape[1] // 2, 0
    for width in widths:
        yield span[:, first : first + 2 * width], span[:, total + first : total + first + 2 * width]
        first += 2 * width


def split_rows(flat):
    high, low = halves_of(flat)
    return jnp.concatenate([high, low], 0), high


def hop_kernel(widths, part, *refs):
    *term, before, span, line, after_rows = refs
    flat = whole_rows(term)
    count = flat.shape[0] // 2
    times_into(line, False, *split_rows(flat), span_pieces(span, widths))
    where = slice(part * count, (part + 1) * count)
    after_rows[0] = before[0, where, :] + flat[:count]
    after_rows[1] = before[1, where, :] + flat[count:]


def hop(term, before, part, count, span, widths):
    shape = (2, count, before.shape[2])
    return pl.pallas_call(
        functools.partial(hop_kernel, widths, part),
        out_shape=[jax.ShapeDtypeStruct(shape, jnp.float32)] * 2,
        compiler_params=pltpu.CompilerParams(vmem_limit_bytes=VMEM_LIMIT),
        cost_estimate=pl.CostEstimate(flops=0, bytes_accessed=0, transcendentals=0),
    )(*term, before, span)


def first_hop_kernel(widths, parts, *refs):
    refs, lines, after_rows = refs[: -parts - 1], refs[-parts - 1 : -1], refs[-1]
    *term, before, span = refs
    flat = whole_rows(term)
    count = flat.shape[0] // 2
    after_rows[0] = before[0] + flat[:count]
    after_rows[1] = before[1] + flat[count:]
    step = count // parts
    for part, line in enumerate(lines):
        where = slice(part * step, (part + 1) * step)
        some = jnp.concatenate([flat[:count][where], flat[count:][where]], 0)
        times_into(line, False, *split_rows(some), span_pieces(span, widths))


def first_hop(term, before, span, widths, parts):
    _, count, bands = before.shape
    shapes = [(2, count // parts, bands)] * parts + [before.shape]
    return pl.pallas_call(
        functools.partial(first_hop_kernel, widths, parts),
        out_shape=[jax.ShapeDtypeStruct(shape, jnp.float32) for shape in shapes],
        compiler_params=pltpu.CompilerParams(vmem_limit_bytes=VMEM_LIMIT),
        cost_estimate=pl.CostEstimate(flops=0, bytes_accessed=0, transcendentals=0),
    )(*term, before, span)


def last_kernel(widths, parts, *refs):
    before, *refs = refs
    received, (*margins, span, out) = refs[:parts], refs[parts:]
    for part, ref in enumerate(received):
        count = ref.shape[1]
        where = slice(part * count, (part + 1) * count)
        reals, imags = before[0, where, :] + ref[0], before[1, where, :] + ref[1]
        both, high = split_rows(jnp.concatenate([reals, imags], 0))
        for i, margin in enumerate(margins):
            times_into(out.at[i, where], True, both, high, [halves_of(margin[...])])
        times_into(out.at[len(margins), where], True, both, high, span_pieces(span, widths))


def last_lines(before, received, span, widths, margins):
    _, count, bands = before.shape
    return pl.pallas_call(
        functools.partial(last_kernel, widths, len(received)),
        out_shape=jax.ShapeDtypeStruct((len(margins) + 1, count, 2, bands), jnp.float32),
        compiler_params=pltpu.CompilerParams(vmem_limit_bytes=VMEM_LIMIT),
        cost_estimate=pl.CostEstimate(flops=0, bytes_accessed=0, transcendentals=0),
    )(before, *received, *margins, span)


def complex_dot(left, right):
    bands = left.shape[0]
    dots = [jnp.dot(left[:, i : i + bands], right, precision=lax.Precision.HIGH) for i in (0, bands)]
    return jnp.concatenate(
        [dots[0][:, :bands] - dots[1][:, bands:], dots[0][:, bands:] + dots[1][:, :bands]], 1
    )


def packed(states, kpoint, first, width):
    return jnp.concatenate([s[kpoint, first : first + width] for s in states], 0)


def after(value, earlier):
    return lax.optimization_barrier((value, earlier))[0]


def other_core(block):
    size = lax.axis_size("pw")
    return lax.ppermute(block, "pw", [(i, i ^ 1) for i in range(size)])


def other_chip(block, distance):
    size = lax.axis_size("pw")
    return lax.ppermute(block, "pw", [(i, (i + 2 * distance) % size) for i in range(size)])


def sum_to_rows(mine, theirs):
    chips = mine.shape[0]
    chip = lax.axis_index("pw") // 2
    half = mine + other_core(theirs)

    def block(place):
        return lax.dynamic_index_in_dim(half, place % chips, 0, keepdims=False)

    received = [other_chip(block(chip + d), d) for d in range(1, chips)]
    return sum(received, block(chip))


def rows_to_core(rows):
    chips = lax.axis_size("pw") // 2
    return jnp.stack([rows] + [other_chip(rows, d) for d in range(1, chips)], 0)


def shards(states_re, states_im):
    kcount, bands, _ = states_re.shape
    ka_width = lax.axis_size("ka")
    pw_width = lax.axis_size("pw")
    band_rows = bands // pw_width
    ka_place = lax.axis_index("ka")
    first_band = lax.axis_index("pw") * band_rows
    core = (lax.axis_index("pw") % 2).reshape(1).astype(jnp.int32)
    place = jnp.stack([lax.axis_index("pw") // 2, lax.axis_index("pw") % 2]).astype(jnp.int32)
    quarter = bands // 4
    widths = [2 * quarter, quarter, quarter]
    firsts = [sum(widths[:i]) for i in range(len(widths))]
    to_previous = [(i, (i - 1) % ka_width) for i in range(ka_width)]
    blocks = [tuple(state[0, : widths[0]] for state in (states_re, states_im))]
    blocks += [packed((states_re, states_im), 0, first, width) for first, width in zip(firsts[1:], widths[1:])]

    def send(number, *earlier):
        return lax.ppermute(after(blocks[number], earlier) if earlier else blocks[number], "ka", to_previous)

    arrivals = [send(0)]
    states = after((states_re, states_im), blocks[0])
    last = kcount - 1
    terms = [margin_section(states, k) for k in range(last)]
    arrivals.append(send(1, terms))
    own_margins = [lax.psum(term, "pw") for term in terms]
    before = own_margins[0]
    for k in range(1, last):
        before = own_margins[k] = complex_dot(before, own_margins[k])
    left = split(after(before, arrivals[0]))

    rows, halves, swapped = [], [], []
    ready = None
    for number in range(len(widths)):
        piece = arrivals[number]
        final = number == len(widths) - 1
        if final:
            reals = [one[:, : one.shape[1] // 2] for one in rows]
            imags = [one[:, one.shape[1] // 2 :] for one in rows]
            ready = lax.ppermute(after(jnp.concatenate(reals + imags, 1), (piece, swapped)), "ka", [(0, 1)])
        if halves:
            piece = after(piece, halves[-1])
        mine, theirs = margin_section(states, last, [piece], left, core)
        if number == 0:
            arrivals.append(send(2, arrivals[0], mine))
        rows.append(sum_to_rows(mine, after(theirs, ready) if final else theirs))
        half = rows_to_core(rows[-1])
        if final:
            received = [ready, lax.ppermute(rows[-1], "ka", [(0, 1)])]
            half = after(half, received[-1])
        halves.append(half)
        swapped.append(other_core(half))
    span = joined(place, halves, swapped)

    row_index = lax.broadcasted_iota(jnp.int32, (band_rows, bands), 0) + first_band
    col_index = lax.broadcasted_iota(jnp.int32, (band_rows, bands), 1)
    eye_real = jnp.where((row_index == col_index) & (ka_place == 0), 1.0, 0.0).astype(jnp.float32)
    start = jnp.stack([eye_real, jnp.zeros_like(eye_real)], 0)
    parts = 2
    *lines, start = first_hop(received, start, span, widths, parts)
    for number in range(1, ka_width - 1):
        received = [lax.ppermute(line, "ka", [(number, number + 1)]) for line in lines]
        if number < ka_width - 2:
            handed = [hop([one], start, part, band_rows // parts, span, widths) for part, one in enumerate(received)]
            lines = [line for line, _ in handed]
            start = jnp.concatenate([rows for _, rows in handed], 1)

    return last_lines(start, received, span, widths, own_margins)


def solution(mesh):
    in_specs = (P("ka", None, "pw"), P("ka", None, "pw"))
    out_specs = P("ka", "pw", None, None)
    return jax.shard_map(shards, mesh=mesh, in_specs=in_specs, out_specs=out_specs, check_vma=False)
```

```python
import functools

import jax
import jax.numpy as jnp
from jax import lax
from jax.experimental import pallas as pl
from jax.experimental.pallas import tpu as pltpu
from jax.sharding import PartitionSpec as P

VMEM_LIMIT = 40 * 1024 * 1024


def halves_of(value):
    high = value.astype(jnp.bfloat16)
    return high, (value - high.astype(jnp.float32)).astype(jnp.bfloat16)


def dot(left, right, across=0):
    return lax.dot_general(left, right, (((1,), (across,)), ((), ())), preferred_element_type=jnp.float32)


def turned(value):
    width = value.shape[1] // 2
    return jnp.concatenate([-value[:, width:], value[:, :width]], 1)


def margin_kernel(steps, pieces, with_left, by_core, *refs):
    refs = list(refs)
    core = refs.pop(0) if by_core else None
    own_re, own_im = refs[:2]
    real_part = jnp.concatenate([ref[...] for ref in refs[2 : 2 + pieces]], 0)
    imag_part = jnp.concatenate([ref[...] for ref in refs[2 + pieces : 2 + 2 * pieces]], 0)
    refs = refs[2 + 2 * pieces :]
    left_high, left_low = refs[:2] if with_left else (None, None)
    outs, total = refs[2 if with_left else 0 : -1], refs[-1]
    step = pl.program_id(0)
    other = jnp.concatenate([jnp.concatenate([real_part, imag_part], 1), jnp.concatenate([imag_part, -real_part], 1)], 0)
    term = dot(jnp.concatenate([own_re[...], own_im[...]], 1), other, 1)

    @pl.when(step == 0)
    def _():
        total[...] = term

    @pl.when(step > 0)
    def _():
        total[...] += term

    @pl.when(step == steps - 1)
    def _():
        if with_left:
            bands = left_high.shape[0]
            value = total[...]
            product = jnp.zeros_like(value)
            for first, factor in ((0, value), (bands, turned(value))):
                high, low = halves_of(factor)
                columns = slice(first, first + bands)
                product += dot(left_high[:, columns], high)
                product += dot(left_high[:, columns], low)
                product += dot(left_low[:, columns], high)
            total[...] = product
        if by_core:
            mine, theirs = outs
            rows = mine.shape[1]
            for chip in range(mine.shape[0]):
                for out, which in ((mine, core[0]), (theirs, 1 - core[0])):
                    first = pl.multiple_of((2 * chip + which) * rows, rows)
                    out[chip] = total[pl.ds(first, rows), :]
        else:
            outs[0][...] = total[...]


def margin_section(states, kpoint, others=None, left=None, core=None):
    _, bands, waves = states[0].shape
    depth = min(1024, waves)
    steps = waves // depth
    own = pl.BlockSpec((None, bands, depth), lambda step: (kpoint, 0, step))
    if others is None:
        width = bands
        other_specs = [pl.BlockSpec((None, bands, depth), lambda step: (kpoint + 1, 0, step))] * 2
        others = states
    else:
        packs = [other if isinstance(other, tuple) else (other, other) for other in others]
        apart = [isinstance(other, tuple) for other in others]
        widths = [pack[0].shape[0] // (1 if one else 2) for pack, one in zip(packs, apart)]
        width = sum(widths)
        other_specs = [pl.BlockSpec((one, depth), lambda step: (0, step)) for one in widths]
        for one, alone in zip(widths, apart):
            other_specs.append(pl.BlockSpec((one, depth), functools.partial(lambda row, step: (row, step), 0 if alone else 1)))
        others = [pack[0] for pack in packs] + [pack[1] for pack in packs]
    operands, specs = [*states, *others], [own, own, *other_specs]
    if left is not None:
        operands += left
        specs += [pl.BlockSpec((bands, 2 * bands), lambda step: (0, 0))] * 2
    if core is not None:
        operands = [core, *operands]
        specs = [pl.BlockSpec(memory_space=pltpu.SMEM), *specs]
        chips = lax.axis_size("pw") // 2
        shape = (chips, bands // (2 * chips), 2 * width)
        out_shape = [jax.ShapeDtypeStruct(shape, jnp.float32)] * 2
        out_specs = [pl.BlockSpec(shape, lambda step: (0, 0, 0))] * 2
    else:
        out_shape = jax.ShapeDtypeStruct((bands, 2 * width), jnp.float32)
        out_specs = pl.BlockSpec((bands, 2 * width), lambda step: (0, 0))
    return pl.pallas_call(
        functools.partial(margin_kernel, steps, len(other_specs) // 2, left is not None, core is not None),
        grid=(steps,),
        in_specs=specs,
        out_specs=out_specs,
        out_shape=out_shape,
        scratch_shapes=[pltpu.VMEM((bands, 2 * width), jnp.float32)],
        compiler_params=pltpu.CompilerParams(vmem_limit_bytes=VMEM_LIMIT),
        cost_estimate=pl.CostEstimate(flops=0, bytes_accessed=0, transcendentals=0),
    )(*operands)


def split_kernel(value, high, low):
    high[...], low[...] = halves_of(value[...])


def split(value):
    return pl.pallas_call(
        split_kernel,
        out_shape=[jax.ShapeDtypeStruct(value.shape, jnp.bfloat16)] * 2,
        compiler_params=pltpu.CompilerParams(vmem_limit_bytes=VMEM_LIMIT),
    )(value)


def whole_rows(term):
    if len(term) == 1 and len(term[0].shape) == 3:
        rows = term[0][...]
        return jnp.concatenate([rows[0], rows[1]], 0)
    widths = [ref.shape[1] // 2 for ref in term]
    reals = [ref[:, :width] for ref, width in zip(term, widths)]
    imags = [ref[:, width:] for ref, width in zip(term, widths)]
    return jnp.concatenate([jnp.concatenate(reals, 1), jnp.concatenate(imags, 1)], 0)


def join_kernel(place, *refs):
    *refs, out = refs
    pairs = len(refs) // 2
    total, first = out.shape[1] // 2, 0
    for mine, theirs in zip(refs[:pairs], refs[pairs:]):
        chips, rows, width = mine.shape
        for chip in range(chips):
            turn = lax.rem(place[0] - chip + chips, chips)
            one, other = mine[turn], theirs[turn]
            for core in (0, 1):
                high, low = halves_of(jnp.where(place[1] == core, one, other))
                where = slice((2 * chip + core) * rows, (2 * chip + core + 1) * rows)
                out[where, first : first + width] = high
                out[where, total + first : total + first + width] = low
        first += width


def joined(place, mine, theirs):
    chips, rows, _ = mine[0].shape
    columns = sum(one.shape[2] for one in mine)
    return pl.pallas_call(
        join_kernel,
        in_specs=[pl.BlockSpec(memory_space=pltpu.SMEM)] + [pl.BlockSpec()] * (2 * len(mine)),
        out_specs=pl.BlockSpec(memory_space=pltpu.VMEM),
        out_shape=jax.ShapeDtypeStruct((2 * chips * rows, 2 * columns), jnp.bfloat16),
        compiler_params=pltpu.CompilerParams(vmem_limit_bytes=VMEM_LIMIT),
        cost_estimate=pl.CostEstimate(flops=0, bytes_accessed=0, transcendentals=0),
    )(place, *mine, *theirs)


def times_into(out, by_row, both, high, pieces):
    count = high.shape[0] // 2
    first = 0
    for piece_high, piece_low in pieces:
        product = dot(both, piece_high)
        product = product[: 2 * count] + product[2 * count :] + dot(high, piece_low)
        width = product.shape[1] // 2
        columns = slice(first, first + width)
        real_part = product[:count, :width] - product[count:, width:]
        imag_part = product[:count, width:] + product[count:, :width]
        if by_row:
            out[:, 0, columns] = real_part
            out[:, 1, columns] = imag_part
        else:
            out[0, :, columns] = real_part
            out[1, :, columns] = imag_part
        first += width


def span_pieces(span, widths):
    total, first = span.shape[1] // 2, 0
    for width in widths:
        yield span[:, first : first + 2 * width], span[:, total + first : total + first + 2 * width]
        first += 2 * width


def split_rows(flat):
    high, low = halves_of(flat)
    return jnp.concatenate([high, low], 0), high


def hop_kernel(widths, part, *refs):
    *term, before, span, line, after_rows = refs
    flat = whole_rows(term)
    count = flat.shape[0] // 2
    times_into(line, False, *split_rows(flat), span_pieces(span, widths))
    where = slice(part * count, (part + 1) * count)
    after_rows[0] = before[0, where, :] + flat[:count]
    after_rows[1] = before[1, where, :] + flat[count:]


def hop(term, before, part, count, span, widths):
    shape = (2, count, before.shape[2])
    return pl.pallas_call(
        functools.partial(hop_kernel, widths, part),
        out_shape=[jax.ShapeDtypeStruct(shape, jnp.float32)] * 2,
        compiler_params=pltpu.CompilerParams(vmem_limit_bytes=VMEM_LIMIT),
        cost_estimate=pl.CostEstimate(flops=0, bytes_accessed=0, transcendentals=0),
    )(*term, before, span)


def first_hop_kernel(widths, parts, *refs):
    refs, lines, after_rows = refs[: -parts - 1], refs[-parts - 1 : -1], refs[-1]
    *term, before, span = refs
    flat = whole_rows(term)
    count = flat.shape[0] // 2
    after_rows[0] = before[0] + flat[:count]
    after_rows[1] = before[1] + flat[count:]
    step = count // parts
    for part, line in enumerate(lines):
        where = slice(part * step, (part + 1) * step)
        some = jnp.concatenate([flat[:count][where], flat[count:][where]], 0)
        times_into(line, False, *split_rows(some), span_pieces(span, widths))


def first_hop(term, before, span, widths, parts):
    _, count, bands = before.shape
    shapes = [(2, count // parts, bands)] * parts + [before.shape]
    return pl.pallas_call(
        functools.partial(first_hop_kernel, widths, parts),
        out_shape=[jax.ShapeDtypeStruct(shape, jnp.float32) for shape in shapes],
        compiler_params=pltpu.CompilerParams(vmem_limit_bytes=VMEM_LIMIT),
        cost_estimate=pl.CostEstimate(flops=0, bytes_accessed=0, transcendentals=0),
    )(*term, before, span)


def last_kernel(widths, parts, *refs):
    before, *refs = refs
    received, (*margins, span, out) = refs[:parts], refs[parts:]
    margins = [halves_of(margin[...]) for margin in margins]
    for part, ref in enumerate(received):
        count = ref.shape[1]
        where = slice(part * count, (part + 1) * count)
        reals, imags = before[0, where, :] + ref[0], before[1, where, :] + ref[1]
        both, high = split_rows(jnp.concatenate([reals, imags], 0))
        for i, margin in enumerate(margins):
            times_into(out.at[i, where], True, both, high, [margin])
        times_into(out.at[len(margins), where], True, both, high, span_pieces(span, widths))


def last_lines(before, received, span, widths, margins):
    _, count, bands = before.shape
    return pl.pallas_call(
        functools.partial(last_kernel, widths, len(received)),
        out_shape=jax.ShapeDtypeStruct((len(margins) + 1, count, 2, bands), jnp.float32),
        compiler_params=pltpu.CompilerParams(vmem_limit_bytes=VMEM_LIMIT),
        cost_estimate=pl.CostEstimate(flops=0, bytes_accessed=0, transcendentals=0),
    )(before, *received, *margins, span)


def complex_dot(left, right):
    bands = left.shape[0]
    dots = [jnp.dot(left[:, i : i + bands], right, precision=lax.Precision.HIGH) for i in (0, bands)]
    return jnp.concatenate(
        [dots[0][:, :bands] - dots[1][:, bands:], dots[0][:, bands:] + dots[1][:, :bands]], 1
    )


def packed(states, kpoint, first, width):
    return jnp.concatenate([s[kpoint, first : first + width] for s in states], 0)


def after(value, earlier):
    return lax.optimization_barrier((value, earlier))[0]


def other_core(block):
    size = lax.axis_size("pw")
    return lax.ppermute(block, "pw", [(i, i ^ 1) for i in range(size)])


def other_chip(block, distance):
    size = lax.axis_size("pw")
    return lax.ppermute(block, "pw", [(i, (i + 2 * distance) % size) for i in range(size)])


def sum_to_rows(mine, theirs):
    chips = mine.shape[0]
    chip = lax.axis_index("pw") // 2
    half = mine + other_core(theirs)

    def block(place):
        return lax.dynamic_index_in_dim(half, place % chips, 0, keepdims=False)

    received = [other_chip(block(chip + d), d) for d in range(1, chips)]
    return sum(received, block(chip))


def rows_to_core(rows):
    chips = lax.axis_size("pw") // 2
    return jnp.stack([rows] + [other_chip(rows, d) for d in range(1, chips)], 0)


def shards(states_re, states_im):
    kcount, bands, _ = states_re.shape
    ka_width = lax.axis_size("ka")
    pw_width = lax.axis_size("pw")
    band_rows = bands // pw_width
    ka_place = lax.axis_index("ka")
    first_band = lax.axis_index("pw") * band_rows
    core = (lax.axis_index("pw") % 2).reshape(1).astype(jnp.int32)
    place = jnp.stack([lax.axis_index("pw") // 2, lax.axis_index("pw") % 2]).astype(jnp.int32)
    quarter = bands // 4
    widths = [2 * quarter, quarter, quarter]
    firsts = [sum(widths[:i]) for i in range(len(widths))]
    to_previous = [(i, (i - 1) % ka_width) for i in range(ka_width)]
    blocks = [tuple(state[0, : widths[0]] for state in (states_re, states_im))]
    blocks += [packed((states_re, states_im), 0, first, width) for first, width in zip(firsts[1:], widths[1:])]

    def send(number, *earlier):
        return lax.ppermute(after(blocks[number], earlier) if earlier else blocks[number], "ka", to_previous)

    arrivals = [send(0)]
    states = after((states_re, states_im), blocks[0])
    last = kcount - 1
    terms = [margin_section(states, k) for k in range(last)]
    arrivals.append(send(1, terms))
    own_margins = [lax.psum(term, "pw") for term in terms]
    before = own_margins[0]
    for k in range(1, last):
        before = own_margins[k] = complex_dot(before, own_margins[k])
    left = split(after(before, arrivals[0]))

    rows, halves, swapped = [], [], []
    ready = None
    for number in range(len(widths)):
        piece = arrivals[number]
        final = number == len(widths) - 1
        if final:
            reals = [one[:, : one.shape[1] // 2] for one in rows]
            imags = [one[:, one.shape[1] // 2 :] for one in rows]
            ready = lax.ppermute(after(jnp.concatenate(reals + imags, 1), swapped), "ka", [(0, 1)])
        if halves:
            piece = after(piece, halves[-1])
        mine, theirs = margin_section(states, last, [piece], left, core)
        if number == 0:
            arrivals.append(send(2, arrivals[0], mine))
        rows.append(sum_to_rows(mine, after(theirs, ready) if final else theirs))
        half = rows_to_core(rows[-1])
        if final:
            received = [ready, lax.ppermute(rows[-1], "ka", [(0, 1)])]
            half = after(half, received[-1])
        halves.append(half)
        swapped.append(other_core(half))
    span = joined(place, halves, swapped)

    row_index = lax.broadcasted_iota(jnp.int32, (band_rows, bands), 0) + first_band
    col_index = lax.broadcasted_iota(jnp.int32, (band_rows, bands), 1)
    eye_real = jnp.where((row_index == col_index) & (ka_place == 0), 1.0, 0.0).astype(jnp.float32)
    start = jnp.stack([eye_real, jnp.zeros_like(eye_real)], 0)
    parts = 2
    *lines, start = first_hop(received, start, span, widths, parts)
    for number in range(1, ka_width - 1):
        received = [lax.ppermute(line, "ka", [(number, number + 1)]) for line in lines]
        if number < ka_width - 2:
            handed = [hop([one], start, part, band_rows // parts, span, widths) for part, one in enumerate(received)]
            lines = [line for line, _ in handed]
            start = jnp.concatenate([rows for _, rows in handed], 1)

    return last_lines(start, received, span, widths, own_margins)


def solution(mesh):
    in_specs = (P("ka", None, "pw"), P("ka", None, "pw"))
    out_specs = P("ka", "pw", None, None)
    return jax.shard_map(shards, mesh=mesh, in_specs=in_specs, out_specs=out_specs, check_vma=False)
```

```python
import functools

import jax
import jax.numpy as jnp
from jax import lax
from jax.experimental import pallas as pl
from jax.experimental.pallas import tpu as pltpu
from jax.sharding import PartitionSpec as P

VMEM_LIMIT = 40 * 1024 * 1024


def halves_of(value):
    high = value.astype(jnp.bfloat16)
    return high, (value - high.astype(jnp.float32)).astype(jnp.bfloat16)


def dot(left, right, across=0):
    return lax.dot_general(left, right, (((1,), (across,)), ((), ())), preferred_element_type=jnp.float32)


def turned(value):
    width = value.shape[1] // 2
    return jnp.concatenate([-value[:, width:], value[:, :width]], 1)


def margin_kernel(steps, pieces, with_left, by_core, *refs):
    refs = list(refs)
    core = refs.pop(0) if by_core else None
    own_re, own_im = refs[:2]
    real_part = jnp.concatenate([ref[...] for ref in refs[2 : 2 + pieces]], 0)
    imag_part = jnp.concatenate([ref[...] for ref in refs[2 + pieces : 2 + 2 * pieces]], 0)
    refs = refs[2 + 2 * pieces :]
    left_high, left_low = refs[:2] if with_left else (None, None)
    outs, total = refs[2 if with_left else 0 : -1], refs[-1]
    step = pl.program_id(0)
    other = jnp.concatenate([jnp.concatenate([real_part, imag_part], 1), jnp.concatenate([imag_part, -real_part], 1)], 0)
    term = dot(jnp.concatenate([own_re[...], own_im[...]], 1), other, 1)

    @pl.when(step == 0)
    def _():
        total[...] = term

    @pl.when(step > 0)
    def _():
        total[...] += term

    @pl.when(step == steps - 1)
    def _():
        if with_left:
            bands = left_high.shape[0]
            value = total[...]
            product = jnp.zeros_like(value)
            for first, factor in ((0, value), (bands, turned(value))):
                high, low = halves_of(factor)
                columns = slice(first, first + bands)
                product += dot(left_high[:, columns], high)
                product += dot(left_high[:, columns], low)
                product += dot(left_low[:, columns], high)
            total[...] = product
        if by_core:
            mine, theirs = outs
            rows = mine.shape[1]
            for chip in range(mine.shape[0]):
                for out, which in ((mine, core[0]), (theirs, 1 - core[0])):
                    first = pl.multiple_of((2 * chip + which) * rows, rows)
                    out[chip] = total[pl.ds(first, rows), :]
        else:
            outs[0][...] = total[...]


def margin_section(states, kpoint, others=None, left=None, core=None):
    _, bands, waves = states[0].shape
    depth = min(1024, waves)
    steps = waves // depth
    own = pl.BlockSpec((None, bands, depth), lambda step: (kpoint, 0, step))
    if others is None:
        width = bands
        other_specs = [pl.BlockSpec((None, bands, depth), lambda step: (kpoint + 1, 0, step))] * 2
        others = states
    else:
        packs = [other if isinstance(other, tuple) else (other, other) for other in others]
        apart = [isinstance(other, tuple) for other in others]
        widths = [pack[0].shape[0] // (1 if one else 2) for pack, one in zip(packs, apart)]
        width = sum(widths)
        other_specs = [pl.BlockSpec((one, depth), lambda step: (0, step)) for one in widths]
        for one, alone in zip(widths, apart):
            other_specs.append(pl.BlockSpec((one, depth), functools.partial(lambda row, step: (row, step), 0 if alone else 1)))
        others = [pack[0] for pack in packs] + [pack[1] for pack in packs]
    operands, specs = [*states, *others], [own, own, *other_specs]
    if left is not None:
        operands += left
        specs += [pl.BlockSpec((bands, 2 * bands), lambda step: (0, 0))] * 2
    if core is not None:
        operands = [core, *operands]
        specs = [pl.BlockSpec(memory_space=pltpu.SMEM), *specs]
        chips = lax.axis_size("pw") // 2
        shape = (chips, bands // (2 * chips), 2 * width)
        out_shape = [jax.ShapeDtypeStruct(shape, jnp.float32)] * 2
        out_specs = [pl.BlockSpec(shape, lambda step: (0, 0, 0))] * 2
    else:
        out_shape = jax.ShapeDtypeStruct((bands, 2 * width), jnp.float32)
        out_specs = pl.BlockSpec((bands, 2 * width), lambda step: (0, 0))
    return pl.pallas_call(
        functools.partial(margin_kernel, steps, len(other_specs) // 2, left is not None, core is not None),
        grid=(steps,),
        in_specs=specs,
        out_specs=out_specs,
        out_shape=out_shape,
        scratch_shapes=[pltpu.VMEM((bands, 2 * width), jnp.float32)],
        compiler_params=pltpu.CompilerParams(vmem_limit_bytes=VMEM_LIMIT),
        cost_estimate=pl.CostEstimate(flops=0, bytes_accessed=0, transcendentals=0),
    )(*operands)


def split_kernel(value, high, low):
    high[...], low[...] = halves_of(value[...])


def split(value):
    return pl.pallas_call(
        split_kernel,
        out_shape=[jax.ShapeDtypeStruct(value.shape, jnp.bfloat16)] * 2,
        compiler_params=pltpu.CompilerParams(vmem_limit_bytes=VMEM_LIMIT),
    )(value)


def whole_rows(term):
    if len(term) == 1 and len(term[0].shape) == 3:
        rows = term[0][...]
        return jnp.concatenate([rows[0], rows[1]], 0)
    widths = [ref.shape[1] // 2 for ref in term]
    reals = [ref[:, :width] for ref, width in zip(term, widths)]
    imags = [ref[:, width:] for ref, width in zip(term, widths)]
    return jnp.concatenate([jnp.concatenate(reals, 1), jnp.concatenate(imags, 1)], 0)


def join_kernel(place, *refs):
    *refs, out = refs
    pairs = len(refs) // 2
    total, first = out.shape[1] // 2, 0
    for mine, theirs in zip(refs[:pairs], refs[pairs:]):
        chips, rows, width = mine.shape
        for chip in range(chips):
            turn = lax.rem(place[0] - chip + chips, chips)
            one, other = mine[turn], theirs[turn]
            for core in (0, 1):
                high, low = halves_of(jnp.where(place[1] == core, one, other))
                where = slice((2 * chip + core) * rows, (2 * chip + core + 1) * rows)
                out[where, first : first + width] = high
                out[where, total + first : total + first + width] = low
        first += width


def joined(place, mine, theirs):
    chips, rows, _ = mine[0].shape
    columns = sum(one.shape[2] for one in mine)
    return pl.pallas_call(
        join_kernel,
        in_specs=[pl.BlockSpec(memory_space=pltpu.SMEM)] + [pl.BlockSpec()] * (2 * len(mine)),
        out_specs=pl.BlockSpec(memory_space=pltpu.VMEM),
        out_shape=jax.ShapeDtypeStruct((2 * chips * rows, 2 * columns), jnp.bfloat16),
        compiler_params=pltpu.CompilerParams(vmem_limit_bytes=VMEM_LIMIT),
        cost_estimate=pl.CostEstimate(flops=0, bytes_accessed=0, transcendentals=0),
    )(place, *mine, *theirs)


def times_into(out, by_row, both, high, pieces):
    count = high.shape[0] // 2
    first = 0
    for piece_high, piece_low in pieces:
        product = dot(both, piece_high)
        product = product[: 2 * count] + product[2 * count :] + dot(high, piece_low)
        width = product.shape[1] // 2
        columns = slice(first, first + width)
        real_part = product[:count, :width] - product[count:, width:]
        imag_part = product[:count, width:] + product[count:, :width]
        if by_row:
            out[:, 0, columns] = real_part
            out[:, 1, columns] = imag_part
        else:
            out[0, :, columns] = real_part
            out[1, :, columns] = imag_part
        first += width


def span_pieces(span, widths):
    total, first = span.shape[1] // 2, 0
    for width in widths:
        yield span[:, first : first + 2 * width], span[:, total + first : total + first + 2 * width]
        first += 2 * width


def split_rows(flat):
    high, low = halves_of(flat)
    return jnp.concatenate([high, low], 0), high


def hop_kernel(widths, part, *refs):
    *term, before, span, line, after_rows = refs
    flat = whole_rows(term)
    count = flat.shape[0] // 2
    times_into(line, False, *split_rows(flat), span_pieces(span, widths))
    where = slice(part * count, (part + 1) * count)
    after_rows[0] = before[0, where, :] + flat[:count]
    after_rows[1] = before[1, where, :] + flat[count:]


def hop(term, before, part, count, span, widths):
    shape = (2, count, before.shape[2])
    return pl.pallas_call(
        functools.partial(hop_kernel, widths, part),
        out_shape=[jax.ShapeDtypeStruct(shape, jnp.float32)] * 2,
        compiler_params=pltpu.CompilerParams(vmem_limit_bytes=VMEM_LIMIT),
        cost_estimate=pl.CostEstimate(flops=0, bytes_accessed=0, transcendentals=0),
    )(*term, before, span)


def first_hop_kernel(widths, parts, *refs):
    refs, lines, after_rows = refs[: -parts - 1], refs[-parts - 1 : -1], refs[-1]
    *term, before, span = refs
    flat = whole_rows(term)
    count = flat.shape[0] // 2
    after_rows[0] = before[0] + flat[:count]
    after_rows[1] = before[1] + flat[count:]
    step = count // parts
    for part, line in enumerate(lines):
        where = slice(part * step, (part + 1) * step)
        some = jnp.concatenate([flat[:count][where], flat[count:][where]], 0)
        times_into(line, False, *split_rows(some), span_pieces(span, widths))


def first_hop(term, before, span, widths, parts):
    _, count, bands = before.shape
    shapes = [(2, count // parts, bands)] * parts + [before.shape]
    return pl.pallas_call(
        functools.partial(first_hop_kernel, widths, parts),
        out_shape=[jax.ShapeDtypeStruct(shape, jnp.float32) for shape in shapes],
        compiler_params=pltpu.CompilerParams(vmem_limit_bytes=VMEM_LIMIT),
        cost_estimate=pl.CostEstimate(flops=0, bytes_accessed=0, transcendentals=0),
    )(*term, before, span)


def last_kernel(widths, parts, *refs):
    before, *refs = refs
    received, (*margins, span, out) = refs[:parts], refs[parts:]
    margins = [halves_of(margin[...]) for margin in margins]
    for part, ref in enumerate(received):
        count = ref.shape[1]
        where = slice(part * count, (part + 1) * count)
        reals, imags = before[0, where, :] + ref[0], before[1, where, :] + ref[1]
        both, high = split_rows(jnp.concatenate([reals, imags], 0))
        for i, margin in enumerate(margins):
            times_into(out.at[i, where], True, both, high, [margin])
        times_into(out.at[len(margins), where], True, both, high, span_pieces(span, widths))


def last_lines(before, received, span, widths, margins):
    _, count, bands = before.shape
    return pl.pallas_call(
        functools.partial(last_kernel, widths, len(received)),
        out_shape=jax.ShapeDtypeStruct((len(margins) + 1, count, 2, bands), jnp.float32),
        compiler_params=pltpu.CompilerParams(vmem_limit_bytes=VMEM_LIMIT),
        cost_estimate=pl.CostEstimate(flops=0, bytes_accessed=0, transcendentals=0),
    )(before, *received, *margins, span)


def complex_dot(left, right):
    bands = left.shape[0]
    dots = [jnp.dot(left[:, i : i + bands], right, precision=lax.Precision.HIGH) for i in (0, bands)]
    return jnp.concatenate(
        [dots[0][:, :bands] - dots[1][:, bands:], dots[0][:, bands:] + dots[1][:, :bands]], 1
    )


def slice_kernel(source, out):
    out[...] = source[...]


def first_bands(state, width):
    waves = state.shape[2]
    step = width // 2
    return pl.pallas_call(
        slice_kernel,
        grid=(2,),
        in_specs=[pl.BlockSpec((None, step, waves), lambda i: (0, i, 0))],
        out_specs=pl.BlockSpec((step, waves), lambda i: (i, 0)),
        out_shape=jax.ShapeDtypeStruct((width, waves), state.dtype),
        compiler_params=pltpu.CompilerParams(vmem_limit_bytes=60 * 1024 * 1024),
    )(state)


def packed(states, kpoint, first, width):
    return jnp.concatenate([s[kpoint, first : first + width] for s in states], 0)


def after(value, earlier):
    return lax.optimization_barrier((value, earlier))[0]


def other_core(block):
    size = lax.axis_size("pw")
    return lax.ppermute(block, "pw", [(i, i ^ 1) for i in range(size)])


def other_chip(block, distance):
    size = lax.axis_size("pw")
    return lax.ppermute(block, "pw", [(i, (i + 2 * distance) % size) for i in range(size)])


def sum_to_rows(mine, theirs):
    chips = mine.shape[0]
    chip = lax.axis_index("pw") // 2
    half = mine + other_core(theirs)

    def block(place):
        return lax.dynamic_index_in_dim(half, place % chips, 0, keepdims=False)

    received = [other_chip(block(chip + d), d) for d in range(1, chips)]
    return sum(received, block(chip))


def rows_to_core(rows):
    chips = lax.axis_size("pw") // 2
    return jnp.stack([rows] + [other_chip(rows, d) for d in range(1, chips)], 0)


def shards(states_re, states_im):
    kcount, bands, _ = states_re.shape
    ka_width = lax.axis_size("ka")
    pw_width = lax.axis_size("pw")
    band_rows = bands // pw_width
    ka_place = lax.axis_index("ka")
    first_band = lax.axis_index("pw") * band_rows
    core = (lax.axis_index("pw") % 2).reshape(1).astype(jnp.int32)
    place = jnp.stack([lax.axis_index("pw") // 2, lax.axis_index("pw") % 2]).astype(jnp.int32)
    quarter = bands // 4
    widths = [2 * quarter, quarter, quarter]
    firsts = [sum(widths[:i]) for i in range(len(widths))]
    to_previous = [(i, (i - 1) % ka_width) for i in range(ka_width)]
    blocks = [tuple(first_bands(state, widths[0]) for state in (states_re, states_im))]
    blocks += [packed((states_re, states_im), 0, first, width) for first, width in zip(firsts[1:], widths[1:])]

    def send(number, *earlier):
        return lax.ppermute(after(blocks[number], earlier) if earlier else blocks[number], "ka", to_previous)

    arrivals = [send(0)]
    states = after((states_re, states_im), blocks[0])
    last = kcount - 1
    terms = [margin_section(states, k) for k in range(last)]
    arrivals.append(send(1, terms))
    own_margins = [lax.psum(term, "pw") for term in terms]
    before = own_margins[0]
    for k in range(1, last):
        before = own_margins[k] = complex_dot(before, own_margins[k])
    left = split(after(before, arrivals[0]))

    rows, halves, swapped = [], [], []
    ready = None
    for number in range(len(widths)):
        piece = arrivals[number]
        final = number == len(widths) - 1
        if final:
            reals = [one[:, : one.shape[1] // 2] for one in rows]
            imags = [one[:, one.shape[1] // 2 :] for one in rows]
            ready = lax.ppermute(after(jnp.concatenate(reals + imags, 1), swapped), "ka", [(0, 1)])
        if halves:
            piece = after(piece, halves[-1])
        mine, theirs = margin_section(states, last, [piece], left, core)
        if number == 0:
            arrivals.append(send(2, arrivals[0], mine))
        rows.append(sum_to_rows(mine, after(theirs, ready) if final else theirs))
        half = rows_to_core(rows[-1])
        if final:
            received = [ready, lax.ppermute(rows[-1], "ka", [(0, 1)])]
            half = after(half, received[-1])
        halves.append(half)
        swapped.append(other_core(half))
    span = joined(place, halves, swapped)

    row_index = lax.broadcasted_iota(jnp.int32, (band_rows, bands), 0) + first_band
    col_index = lax.broadcasted_iota(jnp.int32, (band_rows, bands), 1)
    eye_real = jnp.where((row_index == col_index) & (ka_place == 0), 1.0, 0.0).astype(jnp.float32)
    start = jnp.stack([eye_real, jnp.zeros_like(eye_real)], 0)
    parts = 2
    *lines, start = first_hop(received, start, span, widths, parts)
    for number in range(1, ka_width - 1):
        received = [lax.ppermute(line, "ka", [(number, number + 1)]) for line in lines]
        if number < ka_width - 2:
            handed = [hop([one], start, part, band_rows // parts, span, widths) for part, one in enumerate(received)]
            lines = [line for line, _ in handed]
            start = jnp.concatenate([rows for _, rows in handed], 1)

    return last_lines(start, received, span, widths, own_margins)


def solution(mesh):
    in_specs = (P("ka", None, "pw"), P("ka", None, "pw"))
    out_specs = P("ka", "pw", None, None)
    return jax.shard_map(shards, mesh=mesh, in_specs=in_specs, out_specs=out_specs, check_vma=False)
```

```python
import functools

import jax
import jax.numpy as jnp
from jax import lax
from jax.experimental import pallas as pl
from jax.experimental.pallas import tpu as pltpu
from jax.sharding import PartitionSpec as P

VMEM_LIMIT = 40 * 1024 * 1024


def halves_of(value):
    high = value.astype(jnp.bfloat16)
    return high, (value - high.astype(jnp.float32)).astype(jnp.bfloat16)


def dot(left, right, across=0):
    return lax.dot_general(left, right, (((1,), (across,)), ((), ())), preferred_element_type=jnp.float32)


def turned(value):
    width = value.shape[1] // 2
    return jnp.concatenate([-value[:, width:], value[:, :width]], 1)


def margin_kernel(steps, pieces, with_left, by_core, *refs):
    refs = list(refs)
    core = refs.pop(0) if by_core else None
    own_re, own_im = refs[:2]
    real_part = jnp.concatenate([ref[...] for ref in refs[2 : 2 + pieces]], 0)
    imag_part = jnp.concatenate([ref[...] for ref in refs[2 + pieces : 2 + 2 * pieces]], 0)
    refs = refs[2 + 2 * pieces :]
    left_high, left_low = refs[:2] if with_left else (None, None)
    outs, total = refs[2 if with_left else 0 : -1], refs[-1]
    step = pl.program_id(0)
    other = jnp.concatenate([jnp.concatenate([real_part, imag_part], 1), jnp.concatenate([imag_part, -real_part], 1)], 0)
    term = dot(jnp.concatenate([own_re[...], own_im[...]], 1), other, 1)

    @pl.when(step == 0)
    def _():
        total[...] = term

    @pl.when(step > 0)
    def _():
        total[...] += term

    @pl.when(step == steps - 1)
    def _():
        if with_left:
            bands = left_high.shape[0]
            value = total[...]
            product = jnp.zeros_like(value)
            for first, factor in ((0, value), (bands, turned(value))):
                high, low = halves_of(factor)
                columns = slice(first, first + bands)
                product += dot(left_high[:, columns], high)
                product += dot(left_high[:, columns], low)
                product += dot(left_low[:, columns], high)
            total[...] = product
        if by_core:
            mine, theirs = outs
            rows = mine.shape[1]
            for chip in range(mine.shape[0]):
                for out, which in ((mine, core[0]), (theirs, 1 - core[0])):
                    first = pl.multiple_of((2 * chip + which) * rows, rows)
                    out[chip] = total[pl.ds(first, rows), :]
        else:
            outs[0][...] = total[...]


def margin_section(states, kpoint, others=None, left=None, core=None):
    _, bands, waves = states[0].shape
    depth = min(1024, waves)
    steps = waves // depth
    own = pl.BlockSpec((None, bands, depth), lambda step: (kpoint, 0, step))
    if others is None:
        width = bands
        other_specs = [pl.BlockSpec((None, bands, depth), lambda step: (kpoint + 1, 0, step))] * 2
        others = states
    else:
        packs = [other if isinstance(other, tuple) else (other, other) for other in others]
        apart = [isinstance(other, tuple) for other in others]
        widths = [pack[0].shape[0] // (1 if one else 2) for pack, one in zip(packs, apart)]
        width = sum(widths)
        other_specs = [pl.BlockSpec((one, depth), lambda step: (0, step)) for one in widths]
        for one, alone in zip(widths, apart):
            other_specs.append(pl.BlockSpec((one, depth), functools.partial(lambda row, step: (row, step), 0 if alone else 1)))
        others = [pack[0] for pack in packs] + [pack[1] for pack in packs]
    operands, specs = [*states, *others], [own, own, *other_specs]
    if left is not None:
        operands += left
        specs += [pl.BlockSpec((bands, 2 * bands), lambda step: (0, 0))] * 2
    if core is not None:
        operands = [core, *operands]
        specs = [pl.BlockSpec(memory_space=pltpu.SMEM), *specs]
        chips = lax.axis_size("pw") // 2
        shape = (chips, bands // (2 * chips), 2 * width)
        out_shape = [jax.ShapeDtypeStruct(shape, jnp.float32)] * 2
        out_specs = [pl.BlockSpec(shape, lambda step: (0, 0, 0))] * 2
    else:
        out_shape = jax.ShapeDtypeStruct((bands, 2 * width), jnp.float32)
        out_specs = pl.BlockSpec((bands, 2 * width), lambda step: (0, 0))
    return pl.pallas_call(
        functools.partial(margin_kernel, steps, len(other_specs) // 2, left is not None, core is not None),
        grid=(steps,),
        in_specs=specs,
        out_specs=out_specs,
        out_shape=out_shape,
        scratch_shapes=[pltpu.VMEM((bands, 2 * width), jnp.float32)],
        compiler_params=pltpu.CompilerParams(vmem_limit_bytes=VMEM_LIMIT),
        cost_estimate=pl.CostEstimate(flops=0, bytes_accessed=0, transcendentals=0),
    )(*operands)


def split_kernel(value, high, low):
    high[...], low[...] = halves_of(value[...])


def split(value):
    return pl.pallas_call(
        split_kernel,
        out_shape=[jax.ShapeDtypeStruct(value.shape, jnp.bfloat16)] * 2,
        compiler_params=pltpu.CompilerParams(vmem_limit_bytes=VMEM_LIMIT),
    )(value)


def whole_rows(term):
    if len(term) == 1 and len(term[0].shape) == 3:
        rows = term[0][...]
        return jnp.concatenate([rows[0], rows[1]], 0)
    widths = [ref.shape[1] // 2 for ref in term]
    reals = [ref[:, :width] for ref, width in zip(term, widths)]
    imags = [ref[:, width:] for ref, width in zip(term, widths)]
    return jnp.concatenate([jnp.concatenate(reals, 1), jnp.concatenate(imags, 1)], 0)


def join_kernel(place, *refs):
    *refs, out = refs
    pairs = len(refs) // 2
    total, first = out.shape[1] // 2, 0
    for mine, theirs in zip(refs[:pairs], refs[pairs:]):
        chips, rows, width = mine.shape
        for chip in range(chips):
            turn = lax.rem(place[0] - chip + chips, chips)
            one, other = mine[turn], theirs[turn]
            for core in (0, 1):
                high, low = halves_of(jnp.where(place[1] == core, one, other))
                where = slice((2 * chip + core) * rows, (2 * chip + core + 1) * rows)
                out[where, first : first + width] = high
                out[where, total + first : total + first + width] = low
        first += width


def joined(place, mine, theirs):
    chips, rows, _ = mine[0].shape
    columns = sum(one.shape[2] for one in mine)
    return pl.pallas_call(
        join_kernel,
        in_specs=[pl.BlockSpec(memory_space=pltpu.SMEM)] + [pl.BlockSpec()] * (2 * len(mine)),
        out_specs=pl.BlockSpec(memory_space=pltpu.VMEM),
        out_shape=jax.ShapeDtypeStruct((2 * chips * rows, 2 * columns), jnp.bfloat16),
        compiler_params=pltpu.CompilerParams(vmem_limit_bytes=VMEM_LIMIT),
        cost_estimate=pl.CostEstimate(flops=0, bytes_accessed=0, transcendentals=0),
    )(place, *mine, *theirs)


def times_into(out, by_row, both, high, pieces):
    count = high.shape[0] // 2
    first = 0
    for piece_high, piece_low in pieces:
        product = dot(both, piece_high)
        product = product[: 2 * count] + product[2 * count :] + dot(high, piece_low)
        width = product.shape[1] // 2
        columns = slice(first, first + width)
        real_part = product[:count, :width] - product[count:, width:]
        imag_part = product[:count, width:] + product[count:, :width]
        if by_row:
            out[:, 0, columns] = real_part
            out[:, 1, columns] = imag_part
        else:
            out[0, :, columns] = real_part
            out[1, :, columns] = imag_part
        first += width


def span_pieces(span, widths):
    total, first = span.shape[1] // 2, 0
    for width in widths:
        yield span[:, first : first + 2 * width], span[:, total + first : total + first + 2 * width]
        first += 2 * width


def split_rows(flat):
    high, low = halves_of(flat)
    return jnp.concatenate([high, low], 0), high


def hop_kernel(widths, part, *refs):
    *term, before, span, line, after_rows = refs
    flat = whole_rows(term)
    count = flat.shape[0] // 2
    times_into(line, False, *split_rows(flat), span_pieces(span, widths))
    where = slice(part * count, (part + 1) * count)
    after_rows[0] = before[0, where, :] + flat[:count]
    after_rows[1] = before[1, where, :] + flat[count:]


def hop(term, before, part, count, span, widths):
    shape = (2, count, before.shape[2])
    return pl.pallas_call(
        functools.partial(hop_kernel, widths, part),
        out_shape=[jax.ShapeDtypeStruct(shape, jnp.float32)] * 2,
        compiler_params=pltpu.CompilerParams(vmem_limit_bytes=VMEM_LIMIT),
        cost_estimate=pl.CostEstimate(flops=0, bytes_accessed=0, transcendentals=0),
    )(*term, before, span)


def first_hop_kernel(widths, parts, *refs):
    refs, lines, after_rows = refs[: -parts - 1], refs[-parts - 1 : -1], refs[-1]
    *term, before, span = refs
    flat = whole_rows(term)
    count = flat.shape[0] // 2
    after_rows[0] = before[0] + flat[:count]
    after_rows[1] = before[1] + flat[count:]
    step = count // parts
    for part, line in enumerate(lines):
        where = slice(part * step, (part + 1) * step)
        some = jnp.concatenate([flat[:count][where], flat[count:][where]], 0)
        times_into(line, False, *split_rows(some), span_pieces(span, widths))


def first_hop(term, before, span, widths, parts):
    _, count, bands = before.shape
    shapes = [(2, count // parts, bands)] * parts + [before.shape]
    return pl.pallas_call(
        functools.partial(first_hop_kernel, widths, parts),
        out_shape=[jax.ShapeDtypeStruct(shape, jnp.float32) for shape in shapes],
        compiler_params=pltpu.CompilerParams(vmem_limit_bytes=VMEM_LIMIT),
        cost_estimate=pl.CostEstimate(flops=0, bytes_accessed=0, transcendentals=0),
    )(*term, before, span)


def last_kernel(widths, parts, *refs):
    before, *refs = refs
    received, (*margins, span, out) = refs[:parts], refs[parts:]
    margins = [halves_of(margin[...]) for margin in margins]
    for part, ref in enumerate(received):
        count = ref.shape[1]
        where = slice(part * count, (part + 1) * count)
        reals, imags = before[0, where, :] + ref[0], before[1, where, :] + ref[1]
        both, high = split_rows(jnp.concatenate([reals, imags], 0))
        for i, margin in enumerate(margins):
            times_into(out.at[i, where], True, both, high, [margin])
        times_into(out.at[len(margins), where], True, both, high, span_pieces(span, widths))


def last_lines(before, received, span, widths, margins):
    _, count, bands = before.shape
    return pl.pallas_call(
        functools.partial(last_kernel, widths, len(received)),
        out_shape=jax.ShapeDtypeStruct((len(margins) + 1, count, 2, bands), jnp.float32),
        compiler_params=pltpu.CompilerParams(vmem_limit_bytes=VMEM_LIMIT),
        cost_estimate=pl.CostEstimate(flops=0, bytes_accessed=0, transcendentals=0),
    )(before, *received, *margins, span)


def complex_dot(left, right):
    bands = left.shape[0]
    dots = [jnp.dot(left[:, i : i + bands], right, precision=lax.Precision.HIGH) for i in (0, bands)]
    return jnp.concatenate(
        [dots[0][:, :bands] - dots[1][:, bands:], dots[0][:, bands:] + dots[1][:, :bands]], 1
    )


def slice_kernel(source, out):
    out[...] = source[...]


def first_bands(state, width):
    waves = state.shape[2]
    step = width // 4
    return pl.pallas_call(
        slice_kernel,
        grid=(4,),
        in_specs=[pl.BlockSpec((None, step, waves), lambda i: (0, i, 0))],
        out_specs=pl.BlockSpec((step, waves), lambda i: (i, 0)),
        out_shape=jax.ShapeDtypeStruct((width, waves), state.dtype),
        compiler_params=pltpu.CompilerParams(vmem_limit_bytes=60 * 1024 * 1024),
    )(state)


def packed(states, kpoint, first, width):
    return jnp.concatenate([s[kpoint, first : first + width] for s in states], 0)


def after(value, earlier):
    return lax.optimization_barrier((value, earlier))[0]


def other_core(block):
    size = lax.axis_size("pw")
    return lax.ppermute(block, "pw", [(i, i ^ 1) for i in range(size)])


def other_chip(block, distance):
    size = lax.axis_size("pw")
    return lax.ppermute(block, "pw", [(i, (i + 2 * distance) % size) for i in range(size)])


def sum_to_rows(mine, theirs):
    chips = mine.shape[0]
    chip = lax.axis_index("pw") // 2
    half = mine + other_core(theirs)

    def block(place):
        return lax.dynamic_index_in_dim(half, place % chips, 0, keepdims=False)

    received = [other_chip(block(chip + d), d) for d in range(1, chips)]
    return sum(received, block(chip))


def rows_to_core(rows):
    chips = lax.axis_size("pw") // 2
    return jnp.stack([rows] + [other_chip(rows, d) for d in range(1, chips)], 0)


def shards(states_re, states_im):
    kcount, bands, _ = states_re.shape
    ka_width = lax.axis_size("ka")
    pw_width = lax.axis_size("pw")
    band_rows = bands // pw_width
    ka_place = lax.axis_index("ka")
    first_band = lax.axis_index("pw") * band_rows
    core = (lax.axis_index("pw") % 2).reshape(1).astype(jnp.int32)
    place = jnp.stack([lax.axis_index("pw") // 2, lax.axis_index("pw") % 2]).astype(jnp.int32)
    quarter = bands // 4
    widths = [2 * quarter, quarter, quarter]
    firsts = [sum(widths[:i]) for i in range(len(widths))]
    to_previous = [(i, (i - 1) % ka_width) for i in range(ka_width)]
    blocks = [tuple(first_bands(state, widths[0]) for state in (states_re, states_im))]
    blocks += [packed((states_re, states_im), 0, first, width) for first, width in zip(firsts[1:], widths[1:])]

    def send(number, *earlier):
        return lax.ppermute(after(blocks[number], earlier) if earlier else blocks[number], "ka", to_previous)

    arrivals = [send(0)]
    states = after((states_re, states_im), blocks[0])
    last = kcount - 1
    terms = [margin_section(states, k) for k in range(last)]
    arrivals.append(send(1, terms))
    own_margins = [lax.psum(term, "pw") for term in terms]
    before = own_margins[0]
    for k in range(1, last):
        before = own_margins[k] = complex_dot(before, own_margins[k])
    left = split(after(before, arrivals[0]))

    rows, halves, swapped = [], [], []
    ready = None
    for number in range(len(widths)):
        piece = arrivals[number]
        final = number == len(widths) - 1
        if final:
            reals = [one[:, : one.shape[1] // 2] for one in rows]
            imags = [one[:, one.shape[1] // 2 :] for one in rows]
            ready = lax.ppermute(after(jnp.concatenate(reals + imags, 1), swapped), "ka", [(0, 1)])
        if halves:
            piece = after(piece, halves[-1])
        mine, theirs = margin_section(states, last, [piece], left, core)
        if number == 0:
            arrivals.append(send(2, arrivals[0], mine))
        rows.append(sum_to_rows(mine, after(theirs, ready) if final else theirs))
        half = rows_to_core(rows[-1])
        if final:
            received = [ready, lax.ppermute(rows[-1], "ka", [(0, 1)])]
            half = after(half, received[-1])
        halves.append(half)
        swapped.append(other_core(half))
    span = joined(place, halves, swapped)

    row_index = lax.broadcasted_iota(jnp.int32, (band_rows, bands), 0) + first_band
    col_index = lax.broadcasted_iota(jnp.int32, (band_rows, bands), 1)
    eye_real = jnp.where((row_index == col_index) & (ka_place == 0), 1.0, 0.0).astype(jnp.float32)
    start = jnp.stack([eye_real, jnp.zeros_like(eye_real)], 0)
    parts = 2
    *lines, start = first_hop(received, start, span, widths, parts)
    for number in range(1, ka_width - 1):
        received = [lax.ppermute(line, "ka", [(number, number + 1)]) for line in lines]
        if number < ka_width - 2:
            handed = [hop([one], start, part, band_rows // parts, span, widths) for part, one in enumerate(received)]
            lines = [line for line, _ in handed]
            start = jnp.concatenate([rows for _, rows in handed], 1)

    return last_lines(start, received, span, widths, own_margins)


def solution(mesh):
    in_specs = (P("ka", None, "pw"), P("ka", None, "pw"))
    out_specs = P("ka", "pw", None, None)
    return jax.shard_map(shards, mesh=mesh, in_specs=in_specs, out_specs=out_specs, check_vma=False)
```
